256 devices in a mesh: head: 16 (over z, core), pool: 16 (over y, x).
Axes of the slice: x: 4, y: 4, z: 8, core: 2. Of those that a mesh axis runs over, the one named last changes fastest.
Arguments:
- hidden_in: bfloat16 [64, 16384], P(None, 'pool'), may hold values from -6 to 6
- w_query: bfloat16 [16384, 16384], P('pool', 'head'), may hold values from -0.046875 to 0.046875
- w_key: bfloat16 [16384, 1024], P('pool', 'head'), may hold values from -0.046875 to 0.046875
- w_value: bfloat16 [16384, 1024], P('pool', 'head'), may hold values from -0.046875 to 0.046875
- w_out: bfloat16 [16384, 16384], P('head', 'pool'), may hold values from -0.046875 to 0.046875
- k_cache: bfloat16 [64, 6144, 1024], P('pool', 'head'), may hold values from -110 to 110
- v_cache: bfloat16 [64, 6144, 1024], P('pool', 'head'), may hold values from -6 to 6
- cache_len: int32 [64], replicated, may hold values from 1 to 6144, as said below
- slot_of: int32 [64], replicated, may hold values from 0 to 63, each once
Outputs:
- mixed: float32 [64, 16384], P('head', 'pool')
The draws below stay inside these ranges and needn't reach their ends.
Inputs may be any that keep to these rules, and one draw needn't show every extreme that they name: `slot_of`: every slot holds exactly one request. `cache_len`: one request in every draw has exactly 6144 cached positions.
All inputs are finite; a program needn't handle non-finite values.
Results may differ from the reference program's by a relative error of at most 0.012.
The reference program's roundings to bfloat16 on the way (of `attention`) count: a program that leaves them out, or rounds other values in their place, can miss the bound.
Values may be sent and summed in bfloat16 or wider, within the bound.
A program may use at most 64 MiB of HBM per device.

```python
import math
import jax
import jax.numpy as jnp
from jax import lax

D = 16384
QH = 128
KVH = 8
HD = 128
REQ = 64
MAXLEN = 6144


def draw_k_cache(key, part):
    key = jax.random.fold_in(key, 3)
    key_one = jax.random.fold_in(key, 0)
    dims_full = (REQ, MAXLEN, KVH * HD)
    return (2.0 * jnp.clip(jax.random.normal(key_one, dims_full, jnp.float32), -6.0, 6.0)).astype(jnp.bfloat16)


def draw_cache_len(key, part):
    key = jax.random.fold_in(key, 5)
    key_one, key_two = jax.random.split(key)
    uniform_ints = jax.random.randint(key_one, (REQ,), 1, MAXLEN + 1)
    lengths = jnp.maximum(uniform_ints * uniform_ints // MAXLEN, 1)
    chosen = jax.random.randint(key_two, (), 0, REQ)
    return jnp.where(jnp.arange(REQ) == chosen, MAXLEN, lengths).astype(jnp.int32)


def shard_levels(rng, shape, cuts, smallest, largest):
    loudness, own = 1.0, jax.random.fold_in(rng, 6)
    for dim, shards_of in cuts:
        heights = jnp.exp(jax.random.uniform(jax.random.fold_in(own, dim), (shards_of,), jnp.float32, smallest / len(cuts), largest / len(cuts)))
        loudness = loudness * jnp.repeat(heights, shape[dim] // shards_of).reshape([-1 if axis == dim else 1 for axis in range(len(shape))])
    return loudness


def scatter_about(rng, shape, width, most, cuts=(), held_as=jnp.bfloat16):
    gain = shard_levels(rng, shape, cuts, -0.22, 0.18) if cuts else 1.0
    entries = jax.random.normal(rng, shape, jnp.float32) * width * gain
    return jnp.minimum(jnp.maximum(entries, -most), most).astype(held_as)


def setup_inputs(seed: int = 0) -> dict:
    key_list = jax.random.split(jax.random.key(seed), 10)
    hidden_in = scatter_about(key_list[0], (REQ, D), 1.0, 6.0, ((1, 16),))
    w_query = scatter_about(key_list[1], (D, QH * HD), D ** -0.5, 0.046875, ((0, 16), (1, 16)))
    w_key = scatter_about(key_list[2], (D, KVH * HD), D ** -0.5, 0.046875, ((0, 16), (1, 16)))
    w_value = scatter_about(key_list[3], (D, KVH * HD), D ** -0.5, 0.046875, ((0, 16), (1, 16)))
    w_out = scatter_about(key_list[4], (QH * HD, D), (QH * HD) ** -0.5, 0.046875, ((0, 16), (1, 16)))
    k_cache = draw_k_cache(jax.random.fold_in(key_list[9], 71), 0)
    v_cache = scatter_about(key_list[6], (REQ, MAXLEN, KVH * HD), 1.0, 6.0, ((0, 16), (1, 16)))
    cache_len = draw_cache_len(jax.random.fold_in(key_list[9], 71), 0)
    slot_of = jax.random.permutation(key_list[8], REQ).astype(jnp.int32)
    return {"hidden_in": hidden_in, "w_query": w_query, "w_key": w_key, "w_value": w_value, "w_out": w_out, "k_cache": k_cache, "v_cache": v_cache, "cache_len": cache_len, "slot_of": slot_of}


THETA = 500000.0

def rotate(heads, positions):
    half_dim = heads.shape[-1] // 2
    offsets = jnp.arange(half_dim, dtype=jnp.float32)
    inverse = THETA ** (-2.0 * offsets / heads.shape[-1])
    angles = positions.astype(jnp.float32)[:, None] * inverse[None, :]
    cosine = jnp.cos(angles)[:, None, :]
    sine_part = jnp.sin(angles)[:, None, :]
    leading = heads[..., :half_dim]
    trailing = heads[..., half_dim:]
    return jnp.concatenate([leading * cosine - trailing * sine_part, trailing * cosine + leading * sine_part], axis=-1)

def reference(hidden_in, w_query, w_key, w_value, w_out, k_cache, v_cache, cache_len, slot_of):
    requests = hidden_in.shape[0]
    query = jnp.dot(hidden_in, w_query, preferred_element_type=jnp.float32).reshape(requests, QH, HD)
    key_raw = jnp.dot(hidden_in, w_key, preferred_element_type=jnp.float32).reshape(requests, KVH, HD)
    value_raw = jnp.dot(hidden_in, w_value, preferred_element_type=jnp.float32).reshape(requests, KVH, HD)
    query = lax.optimization_barrier(rotate(query, cache_len).astype(jnp.bfloat16))
    key_new = lax.optimization_barrier(rotate(key_raw, cache_len).astype(jnp.bfloat16))
    value_new = lax.optimization_barrier(value_raw.astype(jnp.bfloat16))
    group_size = QH // KVH
    score_scale = 1.0 / math.sqrt(HD)
    places = jnp.arange(MAXLEN, dtype=jnp.int32)

    def one_request(items):
        query_one, key_one, value_one, slot_one, length_one = items
        slot_one = slot_one.astype(jnp.int32)
        keys_all = lax.dynamic_index_in_dim(k_cache, slot_one, 0, keepdims=False).astype(jnp.float32).reshape(MAXLEN, KVH, HD)
        values_all = lax.dynamic_index_in_dim(v_cache, slot_one, 0, keepdims=False).astype(jnp.float32).reshape(MAXLEN, KVH, HD)
        query_groups = query_one.astype(jnp.float32).reshape(KVH, group_size, HD)
        scores = jnp.einsum('gjd,tgd->gjt', query_groups, keys_all) * score_scale
        own_scores = jnp.einsum('gjd,gd->gj', query_groups, key_one.astype(jnp.float32)) * score_scale
        valid = (places < length_one)[None, None, :]
        top = jnp.maximum(lax.optimization_barrier(jnp.max(jnp.where(valid, scores, -jnp.inf), axis=-1)), own_scores)
        weights = jnp.where(valid, jnp.exp(scores - top[..., None]), 0.0)
        own_weight = jnp.exp(own_scores - top)
        denominator = lax.optimization_barrier(jnp.sum(weights, axis=-1)) + own_weight
        rounded = lax.optimization_barrier(weights.astype(jnp.bfloat16)).astype(jnp.float32)
        own_rounded = lax.optimization_barrier(own_weight.astype(jnp.bfloat16)).astype(jnp.float32)
        numerator = jnp.einsum('gjt,tgd->gjd', rounded, values_all)
        numerator = numerator + own_rounded[..., None] * value_one.astype(jnp.float32)[:, None, :]
        return (numerator / denominator[..., None]).astype(jnp.bfloat16).reshape(QH * HD)
    attention = lax.map(one_request, (query, key_new, value_new, slot_of, cache_len))
    return jnp.dot(attention, w_out, preferred_element_type=jnp.float32)
```

```python
import functools
import math

import jax
import jax.numpy as jnp
import numpy as np
from jax import lax
from jax.experimental import pallas as pl
from jax.experimental.pallas import tpu as pltpu
from jax.sharding import PartitionSpec as P

QH = 128
KVH = 8
HD = 128
THETA = 500000.0
NEGATIVE = -1e30
MESH = pl.DeviceIdType.MESH
F32 = jnp.float32
BF16 = jnp.bfloat16

POOL_OFFSETS = sorted(
    [(dy, dx) for dy in range(4) for dx in range(4) if (dy, dx) != (0, 0)],
    key=lambda o: -(min(o[0], 4 - o[0]) + min(o[1], 4 - o[1])),
)
HEAD_OFFSETS = sorted(
    [(dz, dc) for dz in range(8) for dc in range(2) if (dz, dc) != (0, 0)],
    key=lambda o: -(min(o[0], 8 - o[0]) + 0.5 * o[1]),
)


def pair_rows(x):
    row = lax.broadcasted_iota(jnp.int32, (8, 8, 128), 1)
    left = x[:, :128].reshape(8, 8, 128)
    right = x[:, 128:].reshape(8, 8, 128)
    even = jnp.where(row < 4, left, pltpu.roll(right, 4, 1))
    odd = jnp.where(row < 4, pltpu.roll(left, 4, 1), right)
    return jnp.stack([even, odd], axis=1).reshape(16, 8, 128)


def kernel(
    hid_hbm, wq_hbm, wk_hbm, wv_hbm, wo_hbm, k_hbm, v_hbm, len_ref, slot_ref, inv_ref, out_ref,
    hid, wq, wk, wv, wo, kc, vc,
    s1, r1, qf, s2, r2, skv, rkv, s4, r4, st4, rt4, s5, r5, s6, r6, sel,
    load_sem, send_sem, recv_sem, kv_sem,
):
    head = lax.axis_index("head")
    pool = lax.axis_index("pool")
    z, core = head // 2, head % 2
    py, px = pool // 4, pool % 4

    def pool_peer(offset):
        return lax.rem(py + offset[0], 4) * 4 + lax.rem(px + offset[1], 4)

    def head_peer(offset):
        return lax.rem(z + offset[0], 8) * 2 + lax.rem(core + offset[1], 2)

    def pool_send(src, dst, phase, offset):
        pltpu.make_async_remote_copy(
            src, dst, send_sem.at[phase], recv_sem.at[phase],
            device_id=(head, pool_peer(offset)), device_id_type=MESH,
        ).start()

    def head_send(src, dst, phase, offset):
        pltpu.make_async_remote_copy(
            src, dst, send_sem.at[phase], recv_sem.at[phase],
            device_id=(head_peer(offset), pool), device_id_type=MESH,
        ).start()

    def wait_all(buf, sem):
        pltpu.make_async_copy(buf.at[pl.ds(0, 15)], buf.at[pl.ds(0, 15)], sem).wait()

    loads = [
        pltpu.make_async_copy(hid_hbm, hid, load_sem.at[0]),
        pltpu.make_async_copy(wk_hbm, wk, load_sem.at[1]),
        pltpu.make_async_copy(wv_hbm, wv, load_sem.at[2]),
    ]
    for c in range(4):
        cols = pl.ds(256 * c, 256)
        loads.append(pltpu.make_async_copy(wq_hbm.at[:, cols], wq.at[:, cols], load_sem.at[3 + c]))
    loads.append(pltpu.make_async_copy(k_hbm, kc, load_sem.at[7]))
    loads.append(pltpu.make_async_copy(v_hbm, vc, load_sem.at[8]))
    loads.append(pltpu.make_async_copy(wo_hbm, wo, load_sem.at[9]))
    for copy in loads:
        copy.start()

    barrier = pltpu.get_barrier_semaphore()
    for offset in POOL_OFFSETS:
        pl.semaphore_signal(barrier, inc=1, device_id=(head, pool_peer(offset)), device_id_type=MESH)
    for offset in HEAD_OFFSETS:
        pl.semaphore_signal(barrier, inc=1, device_id=(head_peer(offset), pool), device_id_type=MESH)

    slot_row = slot_ref[...]
    len_row = len_ref[...].astype(F32)
    to_slot = (lax.broadcasted_iota(jnp.int32, (64, 64), 0) == slot_row).astype(BF16)
    mine = pool * 4 + lax.broadcasted_iota(jnp.int32, (8, 64), 0) % 4
    lengths = jnp.sum(jnp.where(mine == slot_row, len_row, 0.0), axis=1, keepdims=True)
    angle = lengths * inv_ref[...]
    lane = lax.broadcasted_iota(jnp.int32, (8, 128), 1)
    cosine = jnp.cos(angle)
    sine = jnp.where(lane < 64, -jnp.sin(angle), jnp.sin(angle))

    def rotate(x):
        return x * cosine + pltpu.roll(x, 64, 1) * sine

    loads[0].wait()
    hidden = jnp.dot(to_slot, hid[...], preferred_element_type=F32).astype(BF16)

    loads[1].wait()
    loads[2].wait()
    zeros = jnp.zeros((64, 64), F32)
    across = (((1,), (1,)), ((), ()))
    key_part = lax.dot_general(hidden, wk[...], across, preferred_element_type=F32)
    value_part = lax.dot_general(hidden, wv[...], across, preferred_element_type=F32)
    s1[:, 32:40, :] = pair_rows(jnp.concatenate([key_part, zeros, value_part, zeros], axis=1))
    for c in range(4):
        loads[3 + c].wait()
        s1[:, 8 * c : 8 * c + 8, :] = pair_rows(
            jnp.dot(hidden, wq[:, 256 * c : 256 * c + 256], preferred_element_type=F32)
        )
    pl.semaphore_wait(barrier, 30)
    for i, offset in enumerate(POOL_OFFSETS):
        pool_send(s1.at[pool_peer(offset)], r1.at[i], 0, offset)

    eye = lax.broadcasted_iota(jnp.int32, (64, 64), 0) == lax.broadcasted_iota(jnp.int32, (64, 64), 1)
    slot_col = jnp.sum(jnp.where(eye, slot_row.astype(F32), 0.0), axis=1, keepdims=True).astype(jnp.int32)
    column = lax.broadcasted_iota(jnp.int32, (64, 512), 1)
    for j in range(8):
        sel[64 * j : 64 * j + 64, :] = (slot_col * 8 + j == column).astype(BF16)

    wait_all(r1, recv_sem.at[0])
    total = s1[pool]
    for i in range(15):
        total = total + r1[i]

    skv[...] = total[32:40]
    kv_copy = pltpu.make_async_remote_copy(
        skv, rkv, kv_sem.at[0], kv_sem.at[1], device_id=(z * 2 + 1 - core, pool), device_id_type=MESH
    )
    for c in range(4):
        qf[8 * c : 8 * c + 8, :] = rotate(total[8 * c : 8 * c + 8])
    query = jnp.concatenate([qf[pl.ds(s, 8, stride=4), :] for s in range(4)], axis=0).astype(BF16)
    s2[...] = query
    r2[head] = query
    for offset in HEAD_OFFSETS:
        head_send(s2, r2.at[head], 1, offset)
    kv_copy.start()
    own_query = query.astype(F32).reshape(4, 8, 128)
    kv_copy.wait()
    here, there = skv[...], rkv[...]
    even = jnp.where(lane < 64, here, pltpu.roll(there, 64, 1))
    odd = jnp.where(lane < 64, there, pltpu.roll(here, 64, 1))
    key_value = jnp.where(core == 0, even, odd)
    key_new = rotate(key_value).astype(BF16).astype(F32)
    value_new = key_value.astype(BF16).astype(F32)
    scale = 1.0 / math.sqrt(HD)
    own = jnp.full((8, 128), NEGATIVE, F32)
    for s in range(4):
        score = jnp.sum(own_query[s] * key_new[s : s + 1, :], axis=1, keepdims=True) * scale
        own = jnp.where(lane == s, score, own)

    wait_all(r2, recv_sem.at[1])
    loads[7].wait()
    loads[8].wait()
    queries = r2[...].astype(F32).reshape(16, 4, 8, 128)
    place = (head * 384 + lax.broadcasted_iota(jnp.int32, (1, 384), 1)).astype(F32)
    wide_lane = lax.broadcasted_iota(jnp.int32, (128, 128), 1)
    stats = jnp.zeros((128, 128), F32)
    sums = []
    for s in range(4):
        q = queries[:, s].reshape(128, 128).astype(BF16)
        scores = jnp.concatenate(
            [
                lax.dot_general(
                    q[16 * g : 16 * g + 16], kc[s, :, 128 * g : 128 * g + 128],
                    across, preferred_element_type=F32,
                )
                for g in range(KVH)
            ],
            axis=0,
        ) * scale
        valid = place < lengths[s : s + 1, :]
        top = jnp.max(jnp.where(valid, scores, NEGATIVE), axis=1, keepdims=True)
        weights = jnp.where(valid, jnp.exp(scores - top), 0.0)
        bottom = jnp.sum(weights, axis=1, keepdims=True)
        weights = weights.astype(BF16)
        sums.append(
            jnp.concatenate(
                [
                    jnp.dot(
                        weights[16 * g : 16 * g + 16], vc[s, :, 128 * g : 128 * g + 128],
                        preferred_element_type=F32,
                    )
                    for g in range(KVH)
                ],
                axis=0,
            ).reshape(16, 8, 128)
        )
        stats = jnp.where(wide_lane == s, top, jnp.where(wide_lane == 4 + s, bottom, stats))

    st4[...] = stats.reshape(16, 8, 128)
    s4[...] = jnp.concatenate(sums, axis=1).astype(BF16)
    for i, offset in enumerate(HEAD_OFFSETS):
        head_send(st4.at[head_peer(offset)], rt4.at[i], 2, offset)
        head_send(s4.at[head_peer(offset)], r4.at[i], 3, offset)
    wait_all(rt4, recv_sem.at[2])
    parts = [rt4[i] for i in range(15)] + [st4[head]]
    largest = own
    for part in parts:
        largest = jnp.maximum(largest, part)
    own_weight = jnp.exp(own - largest)
    denominator = own_weight
    factors = []
    for part in parts:
        factor = jnp.exp(part - largest)
        denominator = denominator + factor * pltpu.roll(part, 124, 1)
        factors.append(factor)
    own_weight = own_weight.astype(BF16).astype(F32)
    numerator = [own_weight[:, s : s + 1] * value_new[4 + s : 5 + s, :] for s in range(4)]
    wait_all(r4, recv_sem.at[3])
    for i in range(16):
        part = (r4[i] if i < 15 else s4[head]).astype(F32)
        for s in range(4):
            numerator[s] = numerator[s] + factors[i][:, s : s + 1] * part[8 * s : 8 * s + 8]
    attention = jnp.concatenate(
        [numerator[s] / denominator[:, s : s + 1] for s in range(4)], axis=0
    ).astype(BF16)

    s5[...] = attention
    r5[pool] = attention
    for offset in POOL_OFFSETS:
        pool_send(s5, r5.at[pool], 4, offset)
    loads[9].wait()
    wait_all(r5, recv_sem.at[4])
    rows = jnp.dot(sel[...], r5[...].reshape(512, 128), preferred_element_type=F32).astype(BF16)
    rows = jnp.concatenate([rows[64 * j : 64 * j + 64] for j in range(8)], axis=1)

    for c in range(2):
        pairs = [
            pair_rows(jnp.dot(rows, wo[:, 256 * i : 256 * i + 256], preferred_element_type=F32))
            for i in (2 * c, 2 * c + 1)
        ]
        s6[:, 16 * c : 16 * c + 16, :] = jnp.concatenate(pairs, axis=1).astype(BF16)
    for i, offset in enumerate(HEAD_OFFSETS):
        head_send(s6.at[head_peer(offset)], r6.at[i], 5, offset)
    wait_all(r6, recv_sem.at[5])
    mixed = s6[head].astype(F32)
    for i in range(15):
        mixed = mixed + r6[i].astype(F32)
    for c in range(4):
        out_ref[:, 256 * c : 256 * c + 128] = mixed[8 * c : 8 * c + 4]
        out_ref[:, 256 * c + 128 : 256 * c + 256] = mixed[8 * c + 4 : 8 * c + 8]

    wait_all(r1, send_sem.at[0])
    wait_all(r2, send_sem.at[1])
    wait_all(rt4, send_sem.at[2])
    wait_all(r4, send_sem.at[3])
    wait_all(r5, send_sem.at[4])
    wait_all(r6, send_sem.at[5])


def local(hidden_in, w_query, w_key, w_value, w_out, k_cache, v_cache, cache_len, slot_of):
    half = np.arange(128) % 64
    inverse = np.broadcast_to((THETA ** (-2.0 * half / HD)).astype(np.float32)[None], (8, 128))
    hbm = pl.BlockSpec(memory_space=pl.ANY)
    vmem = pl.BlockSpec(memory_space=pltpu.VMEM)
    return pl.pallas_call(
        kernel,
        out_shape=jax.ShapeDtypeStruct((4, 1024), F32),
        in_specs=[hbm] * 7 + [vmem] * 3,
        out_specs=vmem,
        scratch_shapes=[
            pltpu.VMEM((64, 1024), BF16),
            pltpu.VMEM((1024, 1024), BF16),
            pltpu.VMEM((64, 1024), BF16),
            pltpu.VMEM((64, 1024), BF16),
            pltpu.VMEM((1024, 1024), BF16),
            pltpu.VMEM((4, 384, 1024), BF16),
            pltpu.VMEM((4, 384, 1024), BF16),
            pltpu.VMEM((16, 40, 128), F32),
            pltpu.VMEM((15, 40, 128), F32),
            pltpu.VMEM((32, 128), F32),
            pltpu.VMEM((32, 128), BF16),
            pltpu.VMEM((16, 32, 128), BF16),
            pltpu.VMEM((8, 128), F32),
            pltpu.VMEM((8, 128), F32),
            pltpu.VMEM((16, 32, 128), BF16),
            pltpu.VMEM((15, 32, 128), BF16),
            pltpu.VMEM((16, 8, 128), F32),
            pltpu.VMEM((15, 8, 128), F32),
            pltpu.VMEM((32, 128), BF16),
            pltpu.VMEM((16, 32, 128), BF16),
            pltpu.VMEM((16, 32, 128), BF16),
            pltpu.VMEM((15, 32, 128), BF16),
            pltpu.VMEM((512, 512), BF16),
            pltpu.SemaphoreType.DMA((10,)),
            pltpu.SemaphoreType.DMA((6,)),
            pltpu.SemaphoreType.DMA((6,)),
            pltpu.SemaphoreType.DMA((2,)),
        ],
        compiler_params=pltpu.CompilerParams(
            collective_id=0, has_side_effects=True, vmem_limit_bytes=48 * 1024 * 1024
        ),
    )(
        hidden_in, w_query, w_key.T, w_value.T, w_out, k_cache, v_cache,
        cache_len.reshape(1, 64), slot_of.reshape(1, 64), jnp.asarray(inverse),
    )


def solution(mesh):
    in_specs = (
        P(None, "pool"),
        P("pool", "head"),
        P("pool", "head"),
        P("pool", "head"),
        P("head", "pool"),
        P("pool", "head", None),
        P("pool", "head", None),
        P(),
        P(),
    )
    out_specs = P("head", "pool")
    return jax.shard_map(local, mesh=mesh, in_specs=in_specs, out_specs=out_specs, check_vma=False)
```

```python
import math

import jax
import jax.numpy as jnp
from jax import lax
from jax.experimental import pallas as pl
from jax.experimental.pallas import tpu as pltpu
from jax.sharding import PartitionSpec as P

QH = 128
KVH = 8
HD = 128
THETA = 500000.0
NEGATIVE = -1e30
MESH = pl.DeviceIdType.MESH
F32 = jnp.float32
BF16 = jnp.bfloat16

POOL_OFFSETS = sorted(
    [(dy, dx) for dy in range(4) for dx in range(4) if (dy, dx) != (0, 0)],
    key=lambda o: -(min(o[0], 4 - o[0]) + min(o[1], 4 - o[1])),
)
HEAD_OFFSETS = sorted(
    [(dz, dc) for dz in range(8) for dc in range(2) if (dz, dc) != (0, 0)],
    key=lambda o: -(min(o[0], 8 - o[0]) + 0.5 * o[1]),
)


def pair_rows(x):
    row = lax.broadcasted_iota(jnp.int32, (8, 8, 128), 1)
    left = x[:, :128].reshape(8, 8, 128)
    right = x[:, 128:].reshape(8, 8, 128)
    even = jnp.where(row < 4, left, pltpu.roll(right, 4, 1))
    odd = jnp.where(row < 4, pltpu.roll(left, 4, 1), right)
    return jnp.stack([even, odd], axis=1).reshape(16, 8, 128)


def kernel(
    hid_hbm, wq_hbm, wk_hbm, wv_hbm, wo_hbm, k_hbm, v_hbm, len_hbm, slot_hbm, out_ref,
    len_ref, slot_ref, hid, wq, wk, wv, wo, kc, vc,
    s1, r1, qf, s2, r2, skv, rkv, s4, r4, st4, rt4, s5, r5, s6, r6, sel,
    load_sem, send_sem, recv_sem, kv_sem,
):
    head = lax.axis_index("head")
    pool = lax.axis_index("pool")
    z, core = head // 2, head % 2
    py, px = pool // 4, pool % 4

    def pool_peer(offset):
        return lax.rem(py + offset[0], 4) * 4 + lax.rem(px + offset[1], 4)

    def head_peer(offset):
        return lax.rem(z + offset[0], 8) * 2 + lax.rem(core + offset[1], 2)

    def pool_send(src, dst, phase, offset):
        pltpu.make_async_remote_copy(
            src, dst, send_sem.at[phase], recv_sem.at[phase],
            device_id=(head, pool_peer(offset)), device_id_type=MESH,
        ).start()

    def head_send(src, dst, phase, offset):
        pltpu.make_async_remote_copy(
            src, dst, send_sem.at[phase], recv_sem.at[phase],
            device_id=(head_peer(offset), pool), device_id_type=MESH,
        ).start()

    def wait_all(buf, sem):
        pltpu.make_async_copy(buf.at[pl.ds(0, 15)], buf.at[pl.ds(0, 15)], sem).wait()

    loads = [
        pltpu.make_async_copy(hid_hbm, hid, load_sem.at[0]),
        pltpu.make_async_copy(wk_hbm, wk, load_sem.at[1]),
        pltpu.make_async_copy(wv_hbm, wv, load_sem.at[2]),
    ]
    for c in range(4):
        cols = pl.ds(256 * c, 256)
        loads.append(pltpu.make_async_copy(wq_hbm.at[:, cols], wq.at[:, cols], load_sem.at[3 + c]))
    loads.append(pltpu.make_async_copy(k_hbm, kc, load_sem.at[7]))
    loads.append(pltpu.make_async_copy(v_hbm, vc, load_sem.at[8]))
    loads.append(pltpu.make_async_copy(wo_hbm, wo, load_sem.at[9]))
    small = [
        pltpu.make_async_copy(len_hbm, len_ref, load_sem.at[10]),
        pltpu.make_async_copy(slot_hbm, slot_ref, load_sem.at[11]),
    ]
    for copy in small + loads:
        copy.start()

    barrier = pltpu.get_barrier_semaphore()
    for offset in POOL_OFFSETS:
        pl.semaphore_signal(barrier, inc=1, device_id=(head, pool_peer(offset)), device_id_type=MESH)
    for offset in HEAD_OFFSETS:
        pl.semaphore_signal(barrier, inc=1, device_id=(head_peer(offset), pool), device_id_type=MESH)

    lane = lax.broadcasted_iota(jnp.int32, (8, 128), 1)
    inverse = jnp.ones((8, 128), F32)
    for bit in range(6):
        step = THETA ** (-2.0 * 2**bit / HD)
        inverse = jnp.where((lane & (1 << bit)) != 0, inverse * step, inverse)

    for copy in small:
        copy.wait()
    slot_row = slot_ref[...]
    len_row = len_ref[...].astype(F32)
    to_slot = (lax.broadcasted_iota(jnp.int32, (64, 64), 0) == slot_row).astype(BF16)
    mine = pool * 4 + lax.broadcasted_iota(jnp.int32, (8, 64), 0) % 4
    lengths = jnp.sum(jnp.where(mine == slot_row, len_row, 0.0), axis=1, keepdims=True)
    angle = lengths * inverse
    cosine = jnp.cos(angle)
    sine = jnp.where(lane < 64, -jnp.sin(angle), jnp.sin(angle))

    def rotate(x):
        return x * cosine + pltpu.roll(x, 64, 1) * sine

    loads[0].wait()
    hidden = jnp.dot(to_slot, hid[...], preferred_element_type=F32).astype(BF16)

    loads[1].wait()
    loads[2].wait()
    zeros = jnp.zeros((64, 64), F32)
    across = (((1,), (1,)), ((), ()))
    key_part = lax.dot_general(hidden, wk[...], across, preferred_element_type=F32)
    value_part = lax.dot_general(hidden, wv[...], across, preferred_element_type=F32)
    s1[:, 32:40, :] = pair_rows(jnp.concatenate([key_part, zeros, value_part, zeros], axis=1))
    for c in range(4):
        loads[3 + c].wait()
        s1[:, 8 * c : 8 * c + 8, :] = pair_rows(
            jnp.dot(hidden, wq[:, 256 * c : 256 * c + 256], preferred_element_type=F32)
        )
    pl.semaphore_wait(barrier, 30)
    for i, offset in enumerate(POOL_OFFSETS):
        pool_send(s1.at[pool_peer(offset)], r1.at[i], 0, offset)

    eye = lax.broadcasted_iota(jnp.int32, (64, 64), 0) == lax.broadcasted_iota(jnp.int32, (64, 64), 1)
    slot_col = jnp.sum(jnp.where(eye, slot_row.astype(F32), 0.0), axis=1, keepdims=True).astype(jnp.int32)
    column = lax.broadcasted_iota(jnp.int32, (64, 512), 1)
    for j in range(8):
        sel[64 * j : 64 * j + 64, :] = (slot_col * 8 + j == column).astype(BF16)

    wait_all(r1, recv_sem.at[0])
    total = s1[pool]
    for i in range(15):
        total = total + r1[i]

    skv[...] = total[32:40]
    kv_copy = pltpu.make_async_remote_copy(
        skv, rkv, kv_sem.at[0], kv_sem.at[1], device_id=(z * 2 + 1 - core, pool), device_id_type=MESH
    )
    for c in range(4):
        qf[8 * c : 8 * c + 8, :] = rotate(total[8 * c : 8 * c + 8])
    query = jnp.concatenate([qf[pl.ds(s, 8, stride=4), :] for s in range(4)], axis=0).astype(BF16)
    s2[...] = query
    r2[head] = query
    for offset in HEAD_OFFSETS:
        head_send(s2, r2.at[head], 1, offset)
    kv_copy.start()
    own_query = query.astype(F32).reshape(4, 8, 128)
    kv_copy.wait()
    here, there = skv[...], rkv[...]
    even = jnp.where(lane < 64, here, pltpu.roll(there, 64, 1))
    odd = jnp.where(lane < 64, there, pltpu.roll(here, 64, 1))
    key_value = jnp.where(core == 0, even, odd)
    key_new = rotate(key_value).astype(BF16).astype(F32)
    value_new = key_value.astype(BF16).astype(F32)
    scale = 1.0 / math.sqrt(HD)
    own = jnp.full((8, 128), NEGATIVE, F32)
    for s in range(4):
        score = jnp.sum(own_query[s] * key_new[s : s + 1, :], axis=1, keepdims=True) * scale
        own = jnp.where(lane == s, score, own)

    wait_all(r2, recv_sem.at[1])
    loads[7].wait()
    loads[8].wait()
    queries = r2[...].astype(F32).reshape(16, 4, 8, 128)
    place = (head * 384 + lax.broadcasted_iota(jnp.int32, (1, 384), 1)).astype(F32)
    wide_lane = lax.broadcasted_iota(jnp.int32, (128, 128), 1)
    stats = jnp.zeros((128, 128), F32)
    sums = []
    for s in range(4):
        q = queries[:, s].reshape(128, 128).astype(BF16)
        scores = jnp.concatenate(
            [
                lax.dot_general(
                    q[16 * g : 16 * g + 16], kc[s, :, 128 * g : 128 * g + 128],
                    across, preferred_element_type=F32,
                )
                for g in range(KVH)
            ],
            axis=0,
        ) * scale
        valid = place < lengths[s : s + 1, :]
        top = jnp.max(jnp.where(valid, scores, NEGATIVE), axis=1, keepdims=True)
        weights = jnp.where(valid, jnp.exp(scores - top), 0.0)
        bottom = jnp.sum(weights, axis=1, keepdims=True)
        weights = weights.astype(BF16)
        sums.append(
            jnp.concatenate(
                [
                    jnp.dot(
                        weights[16 * g : 16 * g + 16], vc[s, :, 128 * g : 128 * g + 128],
                        preferred_element_type=F32,
                    )
                    for g in range(KVH)
                ],
                axis=0,
            ).reshape(16, 8, 128)
        )
        stats = jnp.where(wide_lane == s, top, jnp.where(wide_lane == 4 + s, bottom, stats))

    st4[...] = stats.reshape(16, 8, 128)
    s4[...] = jnp.concatenate(sums, axis=1).astype(BF16)
    for i, offset in enumerate(HEAD_OFFSETS):
        head_send(st4.at[head_peer(offset)], rt4.at[i], 2, offset)
        head_send(s4.at[head_peer(offset)], r4.at[i], 3, offset)
    wait_all(rt4, recv_sem.at[2])
    parts = [rt4[i] for i in range(15)] + [st4[head]]
    largest = own
    for part in parts:
        largest = jnp.maximum(largest, part)
    own_weight = jnp.exp(own - largest)
    denominator = own_weight
    factors = []
    for part in parts:
        factor = jnp.exp(part - largest)
        denominator = denominator + factor * pltpu.roll(part, 124, 1)
        factors.append(factor)
    own_weight = own_weight.astype(BF16).astype(F32)
    numerator = [own_weight[:, s : s + 1] * value_new[4 + s : 5 + s, :] for s in range(4)]
    wait_all(r4, recv_sem.at[3])
    for i in range(16):
        part = (r4[i] if i < 15 else s4[head]).astype(F32)
        for s in range(4):
            numerator[s] = numerator[s] + factors[i][:, s : s + 1] * part[8 * s : 8 * s + 8]
    attention = jnp.concatenate(
        [numerator[s] / denominator[:, s : s + 1] for s in range(4)], axis=0
    ).astype(BF16)

    s5[...] = attention
    r5[pool] = attention
    for offset in POOL_OFFSETS:
        pool_send(s5, r5.at[pool], 4, offset)
    loads[9].wait()
    wait_all(r5, recv_sem.at[4])
    rows = jnp.dot(sel[...], r5[...].reshape(512, 128), preferred_element_type=F32).astype(BF16)
    rows = jnp.concatenate([rows[64 * j : 64 * j + 64] for j in range(8)], axis=1)

    for c in range(2):
        pairs = [
            pair_rows(jnp.dot(rows, wo[:, 256 * i : 256 * i + 256], preferred_element_type=F32))
            for i in (2 * c, 2 * c + 1)
        ]
        s6[:, 16 * c : 16 * c + 16, :] = jnp.concatenate(pairs, axis=1).astype(BF16)
    for i, offset in enumerate(HEAD_OFFSETS):
        head_send(s6.at[head_peer(offset)], r6.at[i], 5, offset)
    wait_all(r6, recv_sem.at[5])
    mixed = s6[head].astype(F32)
    for i in range(15):
        mixed = mixed + r6[i].astype(F32)
    for c in range(4):
        out_ref[:, 256 * c : 256 * c + 128] = mixed[8 * c : 8 * c + 4]
        out_ref[:, 256 * c + 128 : 256 * c + 256] = mixed[8 * c + 4 : 8 * c + 8]

    wait_all(r1, send_sem.at[0])
    wait_all(r2, send_sem.at[1])
    wait_all(rt4, send_sem.at[2])
    wait_all(r4, send_sem.at[3])
    wait_all(r5, send_sem.at[4])
    wait_all(r6, send_sem.at[5])


def local(hidden_in, w_query, w_key, w_value, w_out, k_cache, v_cache, cache_len, slot_of):
    hbm = pl.BlockSpec(memory_space=pl.ANY)
    vmem = pl.BlockSpec(memory_space=pltpu.VMEM)
    return pl.pallas_call(
        kernel,
        out_shape=jax.ShapeDtypeStruct((4, 1024), F32),
        in_specs=[hbm] * 9,
        out_specs=vmem,
        scratch_shapes=[
            pltpu.VMEM((1, 64), jnp.int32),
            pltpu.VMEM((1, 64), jnp.int32),
            pltpu.VMEM((64, 1024), BF16),
            pltpu.VMEM((1024, 1024), BF16),
            pltpu.VMEM((64, 1024), BF16),
            pltpu.VMEM((64, 1024), BF16),
            pltpu.VMEM((1024, 1024), BF16),
            pltpu.VMEM((4, 384, 1024), BF16),
            pltpu.VMEM((4, 384, 1024), BF16),
            pltpu.VMEM((16, 40, 128), F32),
            pltpu.VMEM((15, 40, 128), F32),
            pltpu.VMEM((32, 128), F32),
            pltpu.VMEM((32, 128), BF16),
            pltpu.VMEM((16, 32, 128), BF16),
            pltpu.VMEM((8, 128), F32),
            pltpu.VMEM((8, 128), F32),
            pltpu.VMEM((16, 32, 128), BF16),
            pltpu.VMEM((15, 32, 128), BF16),
            pltpu.VMEM((16, 8, 128), F32),
            pltpu.VMEM((15, 8, 128), F32),
            pltpu.VMEM((32, 128), BF16),
            pltpu.VMEM((16, 32, 128), BF16),
            pltpu.VMEM((16, 32, 128), BF16),
            pltpu.VMEM((15, 32, 128), BF16),
            pltpu.VMEM((512, 512), BF16),
            pltpu.SemaphoreType.DMA((12,)),
            pltpu.SemaphoreType.DMA((6,)),
            pltpu.SemaphoreType.DMA((6,)),
            pltpu.SemaphoreType.DMA((2,)),
        ],
        compiler_params=pltpu.CompilerParams(
            collective_id=0, has_side_effects=True, vmem_limit_bytes=63 * 1024 * 1024
        ),
    )(
        hidden_in, w_query, w_key.T, w_value.T, w_out, k_cache, v_cache,
        cache_len.reshape(1, 64), slot_of.reshape(1, 64),
    )


def solution(mesh):
    in_specs = (
        P(None, "pool"),
        P("pool", "head"),
        P("pool", "head"),
        P("pool", "head"),
        P("head", "pool"),
        P("pool", "head", None),
        P("pool", "head", None),
        P(),
        P(),
    )
    out_specs = P("head", "pool")
    return jax.shard_map(local, mesh=mesh, in_specs=in_specs, out_specs=out_specs, check_vma=False)
```

```python
import math

import jax
import jax.numpy as jnp
from jax import lax
from jax.experimental import pallas as pl
from jax.experimental.pallas import tpu as pltpu
from jax.sharding import PartitionSpec as P

QH = 128
KVH = 8
HD = 128
THETA = 500000.0
NEGATIVE = -1e30
MESH = pl.DeviceIdType.MESH
F32 = jnp.float32
BF16 = jnp.bfloat16
ACROSS = (((1,), (1,)), ((), ()))

POOL_OFFSETS = sorted(
    [(dy, dx) for dy in range(4) for dx in range(4) if (dy, dx) != (0, 0)],
    key=lambda o: -(min(o[0], 4 - o[0]) + min(o[1], 4 - o[1])),
)
HEAD_OFFSETS = sorted(
    [(dz, dc) for dz in range(8) for dc in range(2) if (dz, dc) != (0, 0)],
    key=lambda o: -(min(o[0], 8 - o[0]) + 0.5 * o[1]),
)

BATCHES = ((0, 1, 7), (2, 6), (3, 5), (4,))


def batch_of(dz):
    return next(i for i, steps in enumerate(BATCHES) if dz in steps)


def kernel(
    hid_hbm, wq_hbm, wk_hbm, wv_hbm, wo_hbm, k_hbm, v_hbm, len_hbm, slot_hbm, out_ref,
    len_ref, slot_ref, slot_smem, hid, wq, wkv, wo, kc, vc,
    s1, r1, skv, rkv, swap, s2, r2, s4, r4, st4, rt4, s5, r5, x5, x6, s6, r6,
    load_sem, send_sem, recv_sem, query_sem, swap_sem,
):
    head = lax.axis_index("head")
    pool = lax.axis_index("pool")
    z, core = head // 2, head % 2
    py, px = pool // 4, pool % 4

    def pool_peer(offset):
        return lax.rem(py + offset[0], 4) * 4 + lax.rem(px + offset[1], 4)

    def head_peer(offset):
        return lax.rem(z + offset[0], 8) * 2 + lax.rem(core + offset[1], 2)

    def pool_send(src, dst, phase, offset):
        pltpu.make_async_remote_copy(
            src, dst, send_sem.at[phase], recv_sem.at[phase],
            device_id=(head, pool_peer(offset)), device_id_type=MESH,
        ).start()

    def head_send(src, dst, phase, receive, offset):
        pltpu.make_async_remote_copy(
            src, dst, send_sem.at[phase], receive,
            device_id=(head_peer(offset), pool), device_id_type=MESH,
        ).start()

    def wait_bytes(view, sem):
        pltpu.make_async_copy(view, view, sem).wait()

    def first15(buf):
        return buf.at[pl.ds(0, 15)]

    loads = [
        pltpu.make_async_copy(slot_hbm, slot_ref, load_sem.at[0]),
        pltpu.make_async_copy(hid_hbm, hid, load_sem.at[1]),
    ]
    for c in range(2):
        cols = pl.ds(512 * c, 512)
        loads.append(pltpu.make_async_copy(wq_hbm.at[:, cols], wq.at[:, cols], load_sem.at[2 + c]))
    later = [
        pltpu.make_async_copy(wk_hbm, wkv.at[pl.ds(0, 64)], load_sem.at[6]),
        pltpu.make_async_copy(wv_hbm, wkv.at[pl.ds(64, 64)], load_sem.at[7]),
        pltpu.make_async_copy(len_hbm, len_ref, load_sem.at[8]),
        pltpu.make_async_copy(slot_hbm, slot_smem, load_sem.at[9]),
        pltpu.make_async_copy(k_hbm, kc, load_sem.at[10]),
        pltpu.make_async_copy(v_hbm, vc, load_sem.at[11]),
        pltpu.make_async_copy(wo_hbm, wo, load_sem.at[12]),
    ]
    barrier = pltpu.get_barrier_semaphore()
    for offset in POOL_OFFSETS:
        pl.semaphore_signal(barrier, inc=1, device_id=(head, pool_peer(offset)), device_id_type=MESH)
    for copy in loads:
        copy.start()
    for offset in HEAD_OFFSETS:
        pl.semaphore_signal(barrier, inc=1, device_id=(head_peer(offset), pool), device_id_type=MESH)

    loads[0].wait()
    slot_row = slot_ref[...]
    to_slot = (lax.broadcasted_iota(jnp.int32, (64, 64), 0) == slot_row).astype(BF16)
    loads[1].wait()
    hidden = jnp.dot(to_slot, hid[...], preferred_element_type=F32).astype(BF16)
    for c in range(2):
        loads[2 + c].wait()
        if c == 1:
            for copy in later:
                copy.start()
        part = jnp.dot(hidden, wq[:, 512 * c : 512 * c + 512], preferred_element_type=F32)
        for j in range(4):
            s1[pl.ds(4 * c + j, 64, stride=8), :] = part[:, 128 * j : 128 * j + 128]
    pl.semaphore_wait(barrier, 30)
    for i, offset in enumerate(POOL_OFFSETS):
        rows = pl.ds(pl.multiple_of(32 * pool_peer(offset), 32), 32)
        pool_send(s1.at[rows], r1.at[i], 0, offset)

    later[0].wait()
    later[1].wait()
    key_value = lax.dot_general(hidden, wkv[...], ACROSS, preferred_element_type=F32)
    for p in range(16):
        skv[p] = key_value[4 * p : 4 * p + 4]
    for i, offset in enumerate(POOL_OFFSETS):
        pool_send(skv.at[pool_peer(offset)], rkv.at[i], 1, offset)

    later[2].wait()
    lane = lax.broadcasted_iota(jnp.int32, (8, 128), 1)
    inverse = jnp.ones((8, 128), F32)
    for bit in range(6):
        step = THETA ** (-2.0 * 2**bit / HD)
        inverse = jnp.where((lane & (1 << bit)) != 0, inverse * step, inverse)
    mine = pool * 4 + lax.broadcasted_iota(jnp.int32, (8, 64), 0) % 4
    lengths = jnp.sum(jnp.where(mine == slot_row, len_ref[...].astype(F32), 0.0), axis=1, keepdims=True)
    angle = lengths * inverse
    cosine = jnp.cos(angle)
    sine = jnp.where(lane < 64, -jnp.sin(angle), jnp.sin(angle))

    def rotate(x, rows):
        return x * cosine[rows] + pltpu.roll(x, 64, 1) * sine[rows]

    wait_bytes(r1, recv_sem.at[0])
    total = s1[pl.ds(pl.multiple_of(32 * pool, 32), 32), :]
    for i in range(15):
        total = total + r1[i]

    query = jnp.concatenate(
        [rotate(total[8 * s : 8 * s + 8], slice(s, s + 1)) for s in range(4)], axis=0
    ).astype(BF16)
    s2[...] = query
    for offset in HEAD_OFFSETS[::-1]:
        head_send(s2, r2.at[offset[0], core], 2, query_sem.at[batch_of(offset[0])], offset)
    r2[0, core] = query

    wait_bytes(rkv, recv_sem.at[1])
    here = skv[pool]
    for i in range(15):
        here = here + rkv[i]
    swap[0] = here
    swap_copy = pltpu.make_async_remote_copy(
        swap.at[0], swap.at[1], swap_sem.at[0], swap_sem.at[1],
        device_id=(z * 2 + 1 - core, pool), device_id_type=MESH,
    )
    swap_copy.start()

    scale = 1.0 / math.sqrt(HD)
    later[4].wait()
    later[5].wait()
    place = (head * 384 + lax.broadcasted_iota(jnp.int32, (1, 384), 1)).astype(F32)
    valid = [jnp.broadcast_to(place < lengths[s : s + 1, :], (16, 384)) for s in range(4)]
    row32 = lax.broadcasted_iota(jnp.int32, (32, 128), 0)
    lane32 = lax.broadcasted_iota(jnp.int32, (32, 128), 1)
    for batch, steps in enumerate(BATCHES):
        messages = sum(2 for dz in steps if dz) + (1 if 0 in steps else 0)
        wait_bytes(r4.at[pl.ds(0, messages)], query_sem.at[batch])
        pairs = [(dz, s) for dz in steps for s in range(4)]
        cols = {dz: pl.ds(pl.multiple_of(lax.rem(z + dz, 8) * 128, 128), 128) for dz in steps}
        arrived = {dz: r2[(8 - dz) % 8].astype(F32).reshape(2, 4, 8, 128) for dz in steps}
        scores = [
            lax.dot_general(
                arrived[dz][:, s].reshape(16, 128).astype(BF16), kc[s, :, cols[dz]], ACROSS,
                preferred_element_type=F32,
            ) * scale
            for dz, s in pairs
        ]
        tops = [
            jnp.max(jnp.where(valid[s], x, NEGATIVE), axis=1, keepdims=True)
            for x, (_, s) in zip(scores, pairs)
        ]
        weights = [
            jnp.where(valid[s], jnp.exp(x - top), 0.0) for x, top, (_, s) in zip(scores, tops, pairs)
        ]
        bottoms = [jnp.sum(x, axis=1, keepdims=True) for x in weights]
        sums = [
            jnp.dot(x.astype(BF16), vc[s, :, cols[dz]], preferred_element_type=F32)
            for x, (dz, s) in zip(weights, pairs)
        ]
        for i, dz in enumerate(steps):
            mine = slice(4 * i, 4 * i + 4)
            for c in range(2):
                half = slice(8 * c, 8 * c + 8)
                top = jnp.concatenate([x[half] for x in tops[mine]], axis=0)
                bottom = jnp.concatenate([x[half] for x in bottoms[mine]], axis=0)
                row = jnp.where(row32 == lane32, top, 0.0) + jnp.where(row32 + 32 == lane32, bottom, 0.0)
                st4[dz, c] = jnp.sum(row, axis=0, keepdims=True)
                s4[dz, c] = jnp.concatenate([x[half] for x in sums[mine]], axis=0).astype(BF16)
        for dz in steps:
            for dc in range(2):
                to = lax.rem(core + dc, 2)
                if dz or dc:
                    slot = 2 * dz + dc - 1
                    head_send(st4.at[dz, to], rt4.at[slot], 3, recv_sem.at[3], (dz, dc))
                    head_send(s4.at[dz, to], r4.at[slot], 4, recv_sem.at[4], (dz, dc))
    swap_copy.wait()
    there = swap[1]
    lane4 = lax.broadcasted_iota(jnp.int32, (4, 128), 1)
    here_turned, there_turned = pltpu.roll(here, 64, 1), pltpu.roll(there, 64, 1)
    first = core == 0
    key_raw = jnp.where(lane4 < 64, jnp.where(first, here, there), jnp.where(first, there_turned, here_turned))
    value_raw = jnp.where(lane4 < 64, jnp.where(first, here_turned, there_turned), jnp.where(first, there, here))
    key_new = rotate(key_raw, slice(0, 4)).astype(BF16).astype(F32)
    value_new = value_raw.astype(BF16).astype(F32)

    def spread(x):
        return jnp.concatenate([jnp.broadcast_to(x[s : s + 1], (8, 128)) for s in range(4)], axis=0)

    own = jnp.sum(query.astype(F32) * spread(key_new), axis=1, keepdims=True) * scale
    own = jnp.sum(jnp.where(row32 == lane32, own, 0.0), axis=0, keepdims=True)

    wait_bytes(rt4, recv_sem.at[3])
    parts = jnp.concatenate([rt4[i] for i in range(15)] + [st4[0, core]], axis=0)
    largest = jnp.maximum(jnp.max(parts, axis=0, keepdims=True), own)
    factor = jnp.exp(parts - largest)
    own_weight = jnp.exp(own - largest)
    denominator = jnp.sum(factor * pltpu.roll(parts, 96, 1), axis=0, keepdims=True) + own_weight
    shares = jnp.concatenate(
        [factor / denominator, own_weight.astype(BF16).astype(F32) / denominator, jnp.zeros((111, 128), F32)], axis=0
    ).T
    attention = shares[:32, 16:17] * spread(value_new)
    wait_bytes(r4, recv_sem.at[4])
    for i in range(16):
        part = r4[i] if i < 15 else s4[0, core]
        attention = attention + shares[:32, i : i + 1] * part.astype(F32)
    attention = attention.astype(BF16)

    s5[...] = attention
    for i, offset in enumerate(POOL_OFFSETS):
        pool_send(s5, r5.at[pool], 5, offset)
    r5[pool] = attention
    later[3].wait()
    later[6].wait()
    wait_bytes(first15(r5), recv_sem.at[5])
    x5[...] = r5[...].astype(F32).reshape(512, 128)
    rows = jnp.concatenate([x5[pl.ds(j, 64, stride=8), :].astype(BF16) for j in range(8)], axis=1)

    for c in range(4):
        part = jnp.dot(rows, wo[:, 256 * c : 256 * c + 256], preferred_element_type=F32)
        x6[:, 2 * c, :] = part[:, :128]
        x6[:, 2 * c + 1, :] = part[:, 128:]
    for r in range(0, 64, 2):
        pair = [x6[slot_smem[0, r + i]] for i in range(2)]
        s6[r // 4, 8 * (r % 4) : 8 * (r % 4) + 16, :] = jnp.concatenate(pair, axis=0).astype(BF16)
    for i, offset in enumerate(HEAD_OFFSETS):
        head_send(s6.at[head_peer(offset)], r6.at[i], 6, recv_sem.at[6], offset)
    wait_bytes(r6, recv_sem.at[6])
    mixed = s6[head].astype(F32)
    for i in range(15):
        mixed = mixed + r6[i].astype(F32)
    out_ref[...] = mixed

    wait_bytes(r1, send_sem.at[0])
    wait_bytes(rkv, send_sem.at[1])
    wait_bytes(r4, send_sem.at[2])
    wait_bytes(rt4, send_sem.at[3])
    wait_bytes(r4, send_sem.at[4])
    wait_bytes(first15(r5), send_sem.at[5])
    wait_bytes(r6, send_sem.at[6])


def local(hidden_in, w_query, w_key, w_value, w_out, k_cache, v_cache, cache_len, slot_of):
    hbm = pl.BlockSpec(memory_space=pl.ANY)
    vmem = pl.BlockSpec(memory_space=pltpu.VMEM)
    return pl.pallas_call(
        kernel,
        out_shape=jax.ShapeDtypeStruct((32, 128), F32),
        in_specs=[hbm] * 9,
        out_specs=vmem,
        scratch_shapes=[
            pltpu.VMEM((1, 64), jnp.int32),
            pltpu.VMEM((1, 64), jnp.int32),
            pltpu.SMEM((1, 64), jnp.int32),
            pltpu.VMEM((64, 1024), BF16),
            pltpu.VMEM((1024, 1024), BF16),
            pltpu.VMEM((128, 1024), BF16),
            pltpu.VMEM((1024, 1024), BF16),
            pltpu.VMEM((4, 384, 1024), BF16),
            pltpu.VMEM((4, 384, 1024), BF16),
            pltpu.VMEM((512, 128), F32),
            pltpu.VMEM((15, 32, 128), F32),
            pltpu.VMEM((16, 4, 128), F32),
            pltpu.VMEM((15, 4, 128), F32),
            pltpu.VMEM((2, 4, 128), F32),
            pltpu.VMEM((32, 128), BF16),
            pltpu.VMEM((8, 2, 32, 128), BF16),
            pltpu.VMEM((8, 2, 32, 128), BF16),
            pltpu.VMEM((15, 32, 128), BF16),
            pltpu.VMEM((8, 2, 1, 128), F32),
            pltpu.VMEM((15, 1, 128), F32),
            pltpu.VMEM((32, 128), BF16),
            pltpu.VMEM((16, 32, 128), BF16),
            pltpu.VMEM((512, 128), F32),
            pltpu.VMEM((64, 8, 128), F32),
            pltpu.VMEM((16, 32, 128), BF16),
            pltpu.VMEM((15, 32, 128), BF16),
            pltpu.SemaphoreType.DMA((13,)),
            pltpu.SemaphoreType.DMA((7,)),
            pltpu.SemaphoreType.DMA((7,)),
            pltpu.SemaphoreType.DMA((4,)),
            pltpu.SemaphoreType.DMA((2,)),
        ],
        compiler_params=pltpu.CompilerParams(
            collective_id=0, has_side_effects=True, vmem_limit_bytes=63 * 1024 * 1024
        ),
    )(
        hidden_in, w_query, w_key.T, w_value.T, w_out, k_cache, v_cache,
        cache_len.reshape(1, 64), slot_of.reshape(1, 64),
    ).reshape(4, 1024)


def solution(mesh):
    in_specs = (
        P(None, "pool"),
        P("pool", "head"),
        P("pool", "head"),
        P("pool", "head"),
        P("head", "pool"),
        P("pool", "head", None),
        P("pool", "head", None),
        P(),
        P(),
    )
    out_specs = P("head", "pool")
    return jax.shard_map(local, mesh=mesh, in_specs=in_specs, out_specs=out_specs, check_vma=False)
```

```python
import math

import jax
import jax.numpy as jnp
from jax import lax
from jax.experimental import pallas as pl
from jax.experimental.pallas import tpu as pltpu
from jax.sharding import PartitionSpec as P

QH = 128
KVH = 8
HD = 128
THETA = 500000.0
NEGATIVE = -1e30
MESH = pl.DeviceIdType.MESH
F32 = jnp.float32
BF16 = jnp.bfloat16
ACROSS = (((1,), (1,)), ((), ()))

POOL_OFFSETS = sorted(
    [(dy, dx) for dy in range(4) for dx in range(4) if (dy, dx) != (0, 0)],
    key=lambda o: -(min(o[0], 4 - o[0]) + min(o[1], 4 - o[1])),
)
HEAD_OFFSETS = sorted(
    [(dz, dc) for dz in range(8) for dc in range(2) if (dz, dc) != (0, 0)],
    key=lambda o: -(min(o[0], 8 - o[0]) + 0.5 * o[1]),
)

BATCHES = ((0,), (3,), (1,), (2,))
CHIP_OFFSETS = (1, 7, 2, 6, 3, 5, 4, 0)


def group_slot(dz):
    return ((8 - dz) % 8 - dz % 2) // 2


def kernel(
    hid_hbm, wq_hbm, wk_hbm, wv_hbm, wo_hbm, k_hbm, v_hbm, len_hbm, slot_hbm, out_ref,
    len_ref, slot_ref, slot_smem, hid, wq, wkv, wo, kc, vc,
    s1, r1, skv, rkv, swap, s2, r2, s4, r4, st4, rt4, s5, r5, x5, x6, s6, r6,
    load_sem, send_sem, recv_sem, query_sem, swap_sem, cache_sem,
):
    head = lax.axis_index("head")
    pool = lax.axis_index("pool")
    z, core = head // 2, head % 2
    py, px = pool // 4, pool % 4

    def pool_peer(offset):
        return lax.rem(py + offset[0], 4) * 4 + lax.rem(px + offset[1], 4)

    def head_peer(offset):
        return lax.rem(z + offset[0], 8) * 2 + lax.rem(core + offset[1], 2)

    def pool_send(src, dst, phase, offset):
        pltpu.make_async_remote_copy(
            src, dst, send_sem.at[phase], recv_sem.at[phase],
            device_id=(head, pool_peer(offset)), device_id_type=MESH,
        ).start()

    def head_send(src, dst, phase, receive, offset):
        pltpu.make_async_remote_copy(
            src, dst, send_sem.at[phase], receive,
            device_id=(head_peer(offset), pool), device_id_type=MESH,
        ).start()

    def wait_bytes(view, sem):
        pltpu.make_async_copy(view, view, sem).wait()

    def first15(buf):
        return buf.at[pl.ds(0, 15)]

    loads = [
        pltpu.make_async_copy(slot_hbm, slot_ref, load_sem.at[0]),
        pltpu.make_async_copy(hid_hbm, hid, load_sem.at[1]),
    ]
    for c in range(2):
        cols = pl.ds(512 * c, 512)
        loads.append(pltpu.make_async_copy(wq_hbm.at[:, cols], wq.at[:, cols], load_sem.at[2 + c]))
    later = [
        pltpu.make_async_copy(wk_hbm, wkv.at[pl.ds(0, 64)], load_sem.at[6]),
        pltpu.make_async_copy(wv_hbm, wkv.at[pl.ds(64, 64)], load_sem.at[7]),
        pltpu.make_async_copy(len_hbm, len_ref, load_sem.at[8]),
        pltpu.make_async_copy(slot_hbm, slot_smem, load_sem.at[9]),
    ]
    last = pltpu.make_async_copy(wo_hbm, wo, load_sem.at[10])

    def group_lanes(owner, i):
        return pl.ds(pl.multiple_of(lax.rem(z + owner + 2 * i, 8) * 128, 128), 128)

    kept, given = [], []
    for n, (source, cache) in enumerate(((k_hbm, kc), (v_hbm, vc))):
        for i in range(4):
            kept.append(
                pltpu.make_async_copy(
                    source.at[:, :, group_lanes(core, i)], cache.at[i, core], cache_sem.at[0, 4 * n + i]
                )
            )
            given.append(
                pltpu.make_async_remote_copy(
                    source.at[:, :, group_lanes(1 - core, i)], cache.at[i, core],
                    cache_sem.at[1, 4 * n + i], cache_sem.at[2, 4 * n + i],
                    device_id=(z * 2 + 1 - core, pool), device_id_type=MESH,
                )
            )
    barrier = pltpu.get_barrier_semaphore()
    for offset in POOL_OFFSETS:
        pl.semaphore_signal(barrier, inc=1, device_id=(head, pool_peer(offset)), device_id_type=MESH)
    for copy in loads:
        copy.start()
    for offset in HEAD_OFFSETS:
        pl.semaphore_signal(barrier, inc=1, device_id=(head_peer(offset), pool), device_id_type=MESH)

    loads[0].wait()
    slot_row = slot_ref[...]
    to_slot = (lax.broadcasted_iota(jnp.int32, (64, 64), 0) == slot_row).astype(BF16)
    loads[1].wait()
    hidden = jnp.dot(to_slot, hid[...], preferred_element_type=F32).astype(BF16)
    for c in range(2):
        loads[2 + c].wait()
        if c == 1:
            for copy in later + kept + [last]:
                copy.start()
        part = jnp.dot(hidden, wq[:, 512 * c : 512 * c + 512], preferred_element_type=F32)
        for j in range(4):
            s1[pl.ds(4 * c + j, 64, stride=8), :] = part[:, 128 * j : 128 * j + 128]
    pl.semaphore_wait(barrier, 30)
    for i, offset in enumerate(POOL_OFFSETS):
        rows = pl.ds(pl.multiple_of(32 * pool_peer(offset), 32), 32)
        pool_send(s1.at[rows], r1.at[i], 0, offset)
    for copy in given[:4]:
        copy.start()

    later[0].wait()
    later[1].wait()
    key_value = lax.dot_general(hidden, wkv[...], ACROSS, preferred_element_type=F32)
    for p in range(16):
        skv[p] = key_value[4 * p : 4 * p + 4]
    for i, offset in enumerate(POOL_OFFSETS):
        pool_send(skv.at[pool_peer(offset)], rkv.at[i], 1, offset)
    for copy in given[4:]:
        copy.start()

    later[2].wait()
    lane = lax.broadcasted_iota(jnp.int32, (8, 128), 1)
    inverse = jnp.ones((8, 128), F32)
    for bit in range(6):
        step = THETA ** (-2.0 * 2**bit / HD)
        inverse = jnp.where((lane & (1 << bit)) != 0, inverse * step, inverse)
    mine = pool * 4 + lax.broadcasted_iota(jnp.int32, (8, 64), 0) % 4
    lengths = jnp.sum(jnp.where(mine == slot_row, len_ref[...].astype(F32), 0.0), axis=1, keepdims=True)
    angle = lengths * inverse
    cosine = jnp.cos(angle)
    sine = jnp.where(lane < 64, -jnp.sin(angle), jnp.sin(angle))

    def rotate(x, rows):
        return x * cosine[rows] + pltpu.roll(x, 64, 1) * sine[rows]

    wait_bytes(r1, recv_sem.at[0])
    total = s1[pl.ds(pl.multiple_of(32 * pool, 32), 32), :]
    for i in range(15):
        total = total + r1[i]

    query = jnp.concatenate(
        [rotate(total[8 * s : 8 * s + 8], slice(s, s + 1)) for s in range(4)], axis=0
    ).astype(BF16)
    s2[...] = query
    for dz in CHIP_OFFSETS[:-1]:
        i = group_slot(dz)
        pltpu.make_async_remote_copy(
            s2, r2.at[i, core], send_sem.at[2], query_sem.at[i],
            device_id=(lax.rem(z + dz, 8) * 2 + dz % 2, pool), device_id_type=MESH,
        ).start()

    @pl.when(core == 0)
    def _():
        pltpu.make_async_copy(s2, r2.at[0, 0], query_sem.at[0]).start()

    @pl.when(core == 1)
    def _():
        head_send(s2, r2.at[0, 1], 2, query_sem.at[0], (0, 1))

    wait_bytes(rkv, recv_sem.at[1])
    here = skv[pool]
    for i in range(15):
        here = here + rkv[i]
    swap[0] = here
    swap_copy = pltpu.make_async_remote_copy(
        swap.at[0], swap.at[1], swap_sem.at[0], swap_sem.at[1],
        device_id=(z * 2 + 1 - core, pool), device_id_type=MESH,
    )
    swap_copy.start()

    scale = 1.0 / math.sqrt(HD)
    place = (z * 768 + lax.broadcasted_iota(jnp.int32, (1, 768), 1)).astype(F32)
    valid = [jnp.broadcast_to(place < lengths[s : s + 1, :], (16, 768)) for s in range(4)]
    row32 = lax.broadcasted_iota(jnp.int32, (32, 128), 0)
    lane32 = lax.broadcasted_iota(jnp.int32, (32, 128), 1)
    for batch in BATCHES:
        for i in batch:
            wait_bytes(r2.at[i], query_sem.at[i])
            for n in (i, 4 + i):
                kept[n].wait()
                given[n].wait_recv()
        pairs = [(i, s) for i in batch for s in range(4)]
        arrived = {i: r2[i].astype(F32).reshape(2, 4, 8, 128) for i in batch}
        queries = [arrived[i][:, s].reshape(16, 128).astype(BF16) for i, s in pairs]
        scores = [
            jnp.concatenate(
                [lax.dot_general(q, kc[i, c, s], ACROSS, preferred_element_type=F32) for c in range(2)], axis=1
            ) * scale
            for q, (i, s) in zip(queries, pairs)
        ]
        tops = [
            jnp.max(jnp.where(valid[s], x, NEGATIVE), axis=1, keepdims=True)
            for x, (_, s) in zip(scores, pairs)
        ]
        weights = [
            jnp.where(valid[s], jnp.exp(x - top), 0.0) for x, top, (_, s) in zip(scores, tops, pairs)
        ]
        bottoms = [jnp.sum(x, axis=1, keepdims=True) for x in weights]
        weights = [x.astype(BF16) for x in weights]
        sums = [
            jnp.dot(x[:, :384], vc[i, 0, s], preferred_element_type=F32)
            + jnp.dot(x[:, 384:], vc[i, 1, s], preferred_element_type=F32)
            for x, (i, s) in zip(weights, pairs)
        ]
        for n, i in enumerate(batch):
            mine = slice(4 * n, 4 * n + 4)
            for c in range(2):
                half = slice(8 * c, 8 * c + 8)
                top = jnp.concatenate([x[half] for x in tops[mine]], axis=0)
                bottom = jnp.concatenate([x[half] for x in bottoms[mine]], axis=0)
                row = jnp.where(row32 == lane32, top, 0.0) + jnp.where(row32 + 32 == lane32, bottom, 0.0)
                st4[i, c] = jnp.sum(row, axis=0, keepdims=True)
                s4[i, c] = jnp.concatenate([x[half] for x in sums[mine]], axis=0).astype(BF16)
        for i in batch:
            chip = lax.rem(z + core + 2 * i, 8)
            slot = lax.rem(8 - core - 2 * i + 8, 8)
            for c in range(2):
                remote = [
                    pltpu.make_async_remote_copy(
                        src.at[i, c], dst.at[slot], send_sem.at[phase], recv_sem.at[phase],
                        device_id=(chip * 2 + c, pool), device_id_type=MESH,
                    )
                    for src, dst, phase in ((st4, rt4, 3), (s4, r4, 4))
                ]
                if i or c:
                    for copy in remote:
                        copy.start()
                else:

                    @pl.when(core == 1)
                    def _(remote=remote):
                        for copy in remote:
                            copy.start()

                    @pl.when(core == 0)
                    def _():
                        pltpu.make_async_copy(st4.at[0, 0], rt4.at[0], recv_sem.at[3]).start()
                        pltpu.make_async_copy(s4.at[0, 0], r4.at[0], recv_sem.at[4]).start()

    swap_copy.wait()
    there = swap[1]
    lane4 = lax.broadcasted_iota(jnp.int32, (4, 128), 1)
    here_turned, there_turned = pltpu.roll(here, 64, 1), pltpu.roll(there, 64, 1)
    first = core == 0
    key_raw = jnp.where(lane4 < 64, jnp.where(first, here, there), jnp.where(first, there_turned, here_turned))
    value_raw = jnp.where(lane4 < 64, jnp.where(first, here_turned, there_turned), jnp.where(first, there, here))
    key_new = rotate(key_raw, slice(0, 4)).astype(BF16).astype(F32)
    value_new = value_raw.astype(BF16).astype(F32)

    def spread(x):
        return jnp.concatenate([jnp.broadcast_to(x[s : s + 1], (8, 128)) for s in range(4)], axis=0)

    own = jnp.sum(query.astype(F32) * spread(key_new), axis=1, keepdims=True) * scale
    own = jnp.sum(jnp.where(row32 == lane32, own, 0.0), axis=0, keepdims=True)

    wait_bytes(rt4, recv_sem.at[3])
    parts = jnp.concatenate([rt4[i] for i in range(8)], axis=0)
    largest = jnp.maximum(jnp.max(parts, axis=0, keepdims=True), own)
    factor = jnp.exp(parts - largest)
    own_weight = jnp.exp(own - largest)
    denominator = jnp.sum(factor * pltpu.roll(parts, 96, 1), axis=0, keepdims=True) + own_weight
    shares = jnp.concatenate(
        [factor / denominator, own_weight.astype(BF16).astype(F32) / denominator, jnp.zeros((119, 128), F32)], axis=0
    ).T
    attention = shares[:32, 8:9] * spread(value_new)
    wait_bytes(r4, recv_sem.at[4])
    for i in range(8):
        attention = attention + shares[:32, i : i + 1] * r4[i].astype(F32)
    attention = attention.astype(BF16)

    s5[...] = attention
    for i, offset in enumerate(POOL_OFFSETS):
        pool_send(s5, r5.at[pool], 5, offset)
    r5[pool] = attention
    later[3].wait()
    last.wait()
    wait_bytes(first15(r5), recv_sem.at[5])
    x5[...] = r5[...].astype(F32).reshape(512, 128)
    rows = jnp.concatenate([x5[pl.ds(j, 64, stride=8), :].astype(BF16) for j in range(8)], axis=1)

    for c in range(4):
        part = jnp.dot(rows, wo[:, 256 * c : 256 * c + 256], preferred_element_type=F32)
        x6[:, 2 * c, :] = part[:, :128]
        x6[:, 2 * c + 1, :] = part[:, 128:]
    for r in range(0, 64, 2):
        pair = [x6[slot_smem[0, r + i]] for i in range(2)]
        s6[r // 4, 8 * (r % 4) : 8 * (r % 4) + 16, :] = jnp.concatenate(pair, axis=0).astype(BF16)
    for i, offset in enumerate(HEAD_OFFSETS):
        head_send(s6.at[head_peer(offset)], r6.at[i], 6, recv_sem.at[6], offset)
    wait_bytes(r6, recv_sem.at[6])
    mixed = s6[head].astype(F32)
    for i in range(15):
        mixed = mixed + r6[i].astype(F32)
    out_ref[...] = mixed

    wait_bytes(r1, send_sem.at[0])
    wait_bytes(rkv, send_sem.at[1])
    for copy in given:
        copy.wait_send()
    for buf, phase in ((r4, 2), (rt4, 3), (r4, 4)):
        wait_bytes(buf.at[pl.ds(0, 7)], send_sem.at[phase])

        @pl.when(core == 1)
        def _(buf=buf, phase=phase):
            wait_bytes(buf.at[0], send_sem.at[phase])

    wait_bytes(first15(r5), send_sem.at[5])
    wait_bytes(r6, send_sem.at[6])


def local(hidden_in, w_query, w_key, w_value, w_out, k_cache, v_cache, cache_len, slot_of):
    hbm = pl.BlockSpec(memory_space=pl.ANY)
    vmem = pl.BlockSpec(memory_space=pltpu.VMEM)
    return pl.pallas_call(
        kernel,
        out_shape=pltpu.VMEM((32, 128), F32),
        in_specs=[hbm] * 9,
        out_specs=vmem,
        scratch_shapes=[
            pltpu.VMEM((1, 64), jnp.int32),
            pltpu.VMEM((1, 64), jnp.int32),
            pltpu.SMEM((1, 64), jnp.int32),
            pltpu.VMEM((64, 1024), BF16),
            pltpu.VMEM((1024, 1024), BF16),
            pltpu.VMEM((128, 1024), BF16),
            pltpu.VMEM((1024, 1024), BF16),
            pltpu.VMEM((4, 2, 4, 384, 128), BF16),
            pltpu.VMEM((4, 2, 4, 384, 128), BF16),
            pltpu.VMEM((512, 128), F32),
            pltpu.VMEM((15, 32, 128), F32),
            pltpu.VMEM((16, 4, 128), F32),
            pltpu.VMEM((15, 4, 128), F32),
            pltpu.VMEM((2, 4, 128), F32),
            pltpu.VMEM((32, 128), BF16),
            pltpu.VMEM((4, 2, 32, 128), BF16),
            pltpu.VMEM((4, 2, 32, 128), BF16),
            pltpu.VMEM((8, 32, 128), BF16),
            pltpu.VMEM((4, 2, 1, 128), F32),
            pltpu.VMEM((8, 1, 128), F32),
            pltpu.VMEM((32, 128), BF16),
            pltpu.VMEM((16, 32, 128), BF16),
            pltpu.VMEM((512, 128), F32),
            pltpu.VMEM((64, 8, 128), F32),
            pltpu.VMEM((16, 32, 128), BF16),
            pltpu.VMEM((15, 32, 128), BF16),
            pltpu.SemaphoreType.DMA((11,)),
            pltpu.SemaphoreType.DMA((7,)),
            pltpu.SemaphoreType.DMA((7,)),
            pltpu.SemaphoreType.DMA((4,)),
            pltpu.SemaphoreType.DMA((2,)),
            pltpu.SemaphoreType.DMA((3, 8)),
        ],
        compiler_params=pltpu.CompilerParams(
            collective_id=0, has_side_effects=True, vmem_limit_bytes=63 * 1024 * 1024
        ),
    )(
        hidden_in, w_query, w_key.T, w_value.T, w_out, k_cache, v_cache,
        cache_len.reshape(1, 64), slot_of.reshape(1, 64),
    ).reshape(4, 1024)


def solution(mesh):
    in_specs = (
        P(None, "pool"),
        P("pool", "head"),
        P("pool", "head"),
        P("pool", "head"),
        P("head", "pool"),
        P("pool", "head", None),
        P("pool", "head", None),
        P(),
        P(),
    )
    out_specs = P("head", "pool")
    return jax.shard_map(local, mesh=mesh, in_specs=in_specs, out_specs=out_specs, check_vma=False)
```

```python
import math

import jax
import jax.numpy as jnp
from jax import lax
from jax.experimental import pallas as pl
from jax.experimental.pallas import tpu as pltpu
from jax.sharding import PartitionSpec as P

QH = 128
KVH = 8
HD = 128
THETA = 500000.0
NEGATIVE = -1e30
MESH = pl.DeviceIdType.MESH
F32 = jnp.float32
BF16 = jnp.bfloat16
ACROSS = (((1,), (1,)), ((), ()))

POOL_OFFSETS = sorted(
    [(dy, dx) for dy in range(4) for dx in range(4) if (dy, dx) != (0, 0)],
    key=lambda o: -(min(o[0], 4 - o[0]) + min(o[1], 4 - o[1])),
)
FAR_ROWS = 5
HEAD_OFFSETS = sorted(
    [(dz, dc) for dz in range(8) for dc in range(2) if (dz, dc) != (0, 0)],
    key=lambda o: -(min(o[0], 8 - o[0]) + 0.5 * o[1]),
)
OUTPUT_OFFSETS = sorted(
    HEAD_OFFSETS, key=lambda o: (min(o[0], 8 - o[0]) < 3, -o[1], -min(o[0], 8 - o[0]))
) + [(0, 0)]
FAR_OUTPUTS = 6

BATCHES = ((0,), (3,), (1,), (2,))
CHIP_OFFSETS = (3, 5, 4, 1, 7, 2, 6, 0)


def group_slot(dz):
    return ((8 - dz) % 8 - dz % 2) // 2


def kernel(
    hid_hbm, wq_hbm, wk_hbm, wv_hbm, wo_hbm, k_hbm, v_hbm, len_hbm, slot_hbm, out_ref,
    len_ref, slot_ref, slot_smem, hid, wq, wkv, wo, kc, vc,
    s1, r1, skv, rkv, swap, s2, r2, s4, r4, st4, rt4, s5, r5, x5, x6, s6, r6,
    load_sem, send_sem, recv_sem, query_sem, swap_sem, cache_sem,
):
    head = lax.axis_index("head")
    pool = lax.axis_index("pool")
    z, core = head // 2, head % 2
    py, px = pool // 4, pool % 4

    def pool_peer(offset):
        return lax.rem(py + offset[0], 4) * 4 + lax.rem(px + offset[1], 4)

    def head_peer(offset):
        return lax.rem(z + offset[0], 8) * 2 + lax.rem(core + offset[1], 2)

    def pool_send(src, dst, phase, offset):
        pltpu.make_async_remote_copy(
            src, dst, send_sem.at[phase], recv_sem.at[phase],
            device_id=(head, pool_peer(offset)), device_id_type=MESH,
        ).start()

    def head_send(src, dst, phase, receive, offset):
        pltpu.make_async_remote_copy(
            src, dst, send_sem.at[phase], receive,
            device_id=(head_peer(offset), pool), device_id_type=MESH,
        ).start()

    def wait_bytes(view, sem):
        pltpu.make_async_copy(view, view, sem).wait()

    loads = [
        pltpu.make_async_copy(slot_hbm, slot_ref, load_sem.at[0]),
        pltpu.make_async_copy(hid_hbm, hid, load_sem.at[1]),
    ]
    for c in range(2):
        cols = pl.ds(512 * c, 512)
        loads.append(pltpu.make_async_copy(wq_hbm.at[:, cols], wq.at[:, cols], load_sem.at[2 + c]))
    later = [
        pltpu.make_async_copy(wk_hbm, wkv.at[pl.ds(0, 64)], load_sem.at[6]),
        pltpu.make_async_copy(wv_hbm, wkv.at[pl.ds(64, 64)], load_sem.at[7]),
        pltpu.make_async_copy(len_hbm, len_ref, load_sem.at[8]),
        pltpu.make_async_copy(slot_hbm, slot_smem, load_sem.at[9]),
    ]
    last = pltpu.make_async_copy(wo_hbm, wo, load_sem.at[10])

    def group_lanes(owner, i):
        return pl.ds(pl.multiple_of(lax.rem(z + owner + 2 * i, 8) * 128, 128), 128)

    kept, given = [], []
    for n, (source, cache) in enumerate(((k_hbm, kc), (v_hbm, vc))):
        for i in range(4):
            kept.append(
                pltpu.make_async_copy(
                    source.at[:, :, group_lanes(core, i)], cache.at[i, core], cache_sem.at[0, 4 * n + i]
                )
            )
            given.append(
                pltpu.make_async_remote_copy(
                    source.at[:, :, group_lanes(1 - core, i)], cache.at[i, core],
                    cache_sem.at[1, 4 * n + i], cache_sem.at[2, 4 * n + i],
                    device_id=(z * 2 + 1 - core, pool), device_id_type=MESH,
                )
            )
    barrier = pltpu.get_barrier_semaphore()
    for offset in POOL_OFFSETS:
        pl.semaphore_signal(barrier, inc=1, device_id=(head, pool_peer(offset)), device_id_type=MESH)
    for copy in loads:
        copy.start()
    for offset in HEAD_OFFSETS:
        pl.semaphore_signal(barrier, inc=1, device_id=(head_peer(offset), pool), device_id_type=MESH)

    loads[0].wait()
    slot_row = slot_ref[...]
    to_slot = (lax.broadcasted_iota(jnp.int32, (64, 64), 0) == slot_row).astype(BF16)
    loads[1].wait()
    hidden = jnp.dot(to_slot, hid[...], preferred_element_type=F32).astype(BF16)
    for c in range(2):
        loads[2 + c].wait()
        if c == 1:
            for copy in later + kept + [last]:
                copy.start()
        part = jnp.dot(hidden, wq[:, 512 * c : 512 * c + 512], preferred_element_type=F32)
        for j in range(4):
            s1[pl.ds(4 * c + j, 64, stride=8), :] = part[:, 128 * j : 128 * j + 128]
    pl.semaphore_wait(barrier, 30)
    for i, offset in enumerate(POOL_OFFSETS):
        rows = pl.ds(pl.multiple_of(32 * pool_peer(offset), 32), 32)
        pool_send(s1.at[rows], r1.at[i], 0, offset)
    for copy in given[:4]:
        copy.start()

    later[0].wait()
    later[1].wait()
    key_value = lax.dot_general(hidden, wkv[...], ACROSS, preferred_element_type=F32)
    for p in range(16):
        skv[p] = key_value[4 * p : 4 * p + 4]
    for copy in given[4:]:
        copy.start()

    later[2].wait()
    lane = lax.broadcasted_iota(jnp.int32, (8, 128), 1)
    inverse = jnp.ones((8, 128), F32)
    for bit in range(6):
        step = THETA ** (-2.0 * 2**bit / HD)
        inverse = jnp.where((lane & (1 << bit)) != 0, inverse * step, inverse)
    mine = pool * 4 + lax.broadcasted_iota(jnp.int32, (8, 64), 0) % 4
    lengths = jnp.sum(jnp.where(mine == slot_row, len_ref[...].astype(F32), 0.0), axis=1, keepdims=True)
    angle = lengths * inverse
    cosine = jnp.cos(angle)
    sine = jnp.where(lane < 64, -jnp.sin(angle), jnp.sin(angle))

    def rotate(x, rows):
        return x * cosine[rows] + pltpu.roll(x, 64, 1) * sine[rows]

    wait_bytes(r1, recv_sem.at[0])
    total = s1[pl.ds(pl.multiple_of(32 * pool, 32), 32), :]
    for i in range(15):
        total = total + r1[i]

    query = jnp.concatenate(
        [rotate(total[8 * s : 8 * s + 8], slice(s, s + 1)) for s in range(4)], axis=0
    ).astype(BF16)
    s2[...] = query
    for dz in CHIP_OFFSETS[:-1]:
        i = group_slot(dz)
        pltpu.make_async_remote_copy(
            s2, r2.at[i, core], send_sem.at[2], query_sem.at[i],
            device_id=(lax.rem(z + dz, 8) * 2 + dz % 2, pool), device_id_type=MESH,
        ).start()

    @pl.when(core == 0)
    def _():
        pltpu.make_async_copy(s2, r2.at[0, 0], query_sem.at[0]).start()

    @pl.when(core == 1)
    def _():
        head_send(s2, r2.at[0, 1], 2, query_sem.at[0], (0, 1))

    for i, offset in enumerate(POOL_OFFSETS):
        pool_send(skv.at[pool_peer(offset)], rkv.at[i], 1, offset)

    scale = 1.0 / math.sqrt(HD)
    place = (z * 768 + lax.broadcasted_iota(jnp.int32, (1, 768), 1)).astype(F32)
    valid = [jnp.broadcast_to(place < lengths[s : s + 1, :], (16, 768)) for s in range(4)]
    row32 = lax.broadcasted_iota(jnp.int32, (32, 128), 0)
    lane32 = lax.broadcasted_iota(jnp.int32, (32, 128), 1)
    for batch in BATCHES:
        if batch == BATCHES[-1]:
            wait_bytes(rkv, recv_sem.at[1])
            here = skv[pool]
            for i in range(15):
                here = here + rkv[i]
            swap[0] = here
            swap_copy = pltpu.make_async_remote_copy(
                swap.at[0], swap.at[1], swap_sem.at[0], swap_sem.at[1],
                device_id=(z * 2 + 1 - core, pool), device_id_type=MESH,
            )
            swap_copy.start()
        for i in batch:
            wait_bytes(r2.at[i], query_sem.at[i])
            for n in (i, 4 + i):
                kept[n].wait()
                given[n].wait_recv()
        pairs = [(i, s) for i in batch for s in range(4)]
        arrived = {i: r2[i].astype(F32).reshape(2, 4, 8, 128) for i in batch}
        queries = [arrived[i][:, s].reshape(16, 128).astype(BF16) for i, s in pairs]
        scores = [
            jnp.concatenate(
                [lax.dot_general(q, kc[i, c, s], ACROSS, preferred_element_type=F32) for c in range(2)], axis=1
            ) * scale
            for q, (i, s) in zip(queries, pairs)
        ]
        tops = [
            jnp.max(jnp.where(valid[s], x, NEGATIVE), axis=1, keepdims=True)
            for x, (_, s) in zip(scores, pairs)
        ]
        weights = [
            jnp.where(valid[s], jnp.exp(x - top), 0.0) for x, top, (_, s) in zip(scores, tops, pairs)
        ]
        bottoms = [jnp.sum(x, axis=1, keepdims=True) for x in weights]
        weights = [x.astype(BF16) for x in weights]
        sums = [
            jnp.dot(x[:, :384], vc[i, 0, s], preferred_element_type=F32)
            + jnp.dot(x[:, 384:], vc[i, 1, s], preferred_element_type=F32)
            for x, (i, s) in zip(weights, pairs)
        ]
        for n, i in enumerate(batch):
            mine = slice(4 * n, 4 * n + 4)
            for c in range(2):
                half = slice(8 * c, 8 * c + 8)
                top = jnp.concatenate([x[half] for x in tops[mine]], axis=0)
                bottom = jnp.concatenate([x[half] for x in bottoms[mine]], axis=0)
                row = jnp.where(row32 == lane32, top, 0.0) + jnp.where(row32 + 32 == lane32, bottom, 0.0)
                st4[i, c] = jnp.sum(row, axis=0, keepdims=True)
                s4[i, c] = jnp.concatenate([x[half] for x in sums[mine]], axis=0).astype(BF16)
        for i in batch:
            chip = lax.rem(z + core + 2 * i, 8)
            slot = lax.rem(8 - core - 2 * i + 8, 8)
            for c in range(2):
                remote = [
                    pltpu.make_async_remote_copy(
                        src.at[i, c], dst.at[slot], send_sem.at[phase], recv_sem.at[phase],
                        device_id=(chip * 2 + c, pool), device_id_type=MESH,
                    )
                    for src, dst, phase in ((st4, rt4, 3), (s4, r4, 4))
                ]
                if i or c:
                    for copy in remote:
                        copy.start()
                else:

                    @pl.when(core == 1)
                    def _(remote=remote):
                        for copy in remote:
                            copy.start()

                    @pl.when(core == 0)
                    def _():
                        pltpu.make_async_copy(st4.at[0, 0], rt4.at[0], recv_sem.at[3]).start()
                        pltpu.make_async_copy(s4.at[0, 0], r4.at[0], recv_sem.at[4]).start()

    swap_copy.wait()
    there = swap[1]
    lane4 = lax.broadcasted_iota(jnp.int32, (4, 128), 1)
    here_turned, there_turned = pltpu.roll(here, 64, 1), pltpu.roll(there, 64, 1)
    first = core == 0
    key_raw = jnp.where(lane4 < 64, jnp.where(first, here, there), jnp.where(first, there_turned, here_turned))
    value_raw = jnp.where(lane4 < 64, jnp.where(first, here_turned, there_turned), jnp.where(first, there, here))
    key_new = rotate(key_raw, slice(0, 4)).astype(BF16).astype(F32)
    value_new = value_raw.astype(BF16).astype(F32)

    def spread(x):
        return jnp.concatenate([jnp.broadcast_to(x[s : s + 1], (8, 128)) for s in range(4)], axis=0)

    own = jnp.sum(query.astype(F32) * spread(key_new), axis=1, keepdims=True) * scale
    own = jnp.sum(jnp.where(row32 == lane32, own, 0.0), axis=0, keepdims=True)

    wait_bytes(rt4, recv_sem.at[3])
    parts = jnp.concatenate([rt4[i] for i in range(8)], axis=0)
    largest = jnp.maximum(jnp.max(parts, axis=0, keepdims=True), own)
    factor = jnp.exp(parts - largest)
    own_weight = jnp.exp(own - largest)
    denominator = jnp.sum(factor * pltpu.roll(parts, 96, 1), axis=0, keepdims=True) + own_weight
    shares = jnp.concatenate(
        [factor / denominator, own_weight.astype(BF16).astype(F32) / denominator, jnp.zeros((119, 128), F32)], axis=0
    ).T
    attention = shares[:32, 8:9] * spread(value_new)
    wait_bytes(r4, recv_sem.at[4])
    for i in range(8):
        attention = attention + shares[:32, i : i + 1] * r4[i].astype(F32)
    attention = attention.astype(BF16)

    s5[...] = attention
    for i, offset in enumerate(POOL_OFFSETS):
        pltpu.make_async_remote_copy(
            s5, r5.at[i], send_sem.at[5], recv_sem.at[5 if i < FAR_ROWS else 8],
            device_id=(head, pool_peer(offset)), device_id_type=MESH,
        ).start()
    later[3].wait()
    last.wait()

    def place_rows(source, block):
        x5[pl.ds(pl.multiple_of(source * 32, 32), 32), :] = block.astype(F32)

    place_rows(pool, s5[...])
    wait_bytes(r5.at[pl.ds(FAR_ROWS, 15 - FAR_ROWS)], recv_sem.at[8])
    for i in range(FAR_ROWS, 15):
        place_rows(pool_peer([4 - o for o in POOL_OFFSETS[i]]), r5[i])
    wait_bytes(r5.at[pl.ds(0, FAR_ROWS)], recv_sem.at[5])
    for i in range(FAR_ROWS):
        place_rows(pool_peer([4 - o for o in POOL_OFFSETS[i]]), r5[i])
    rows = jnp.concatenate([x5[pl.ds(j, 64, stride=8), :].astype(BF16) for j in range(8)], axis=1)

    for c in range(4):
        part = jnp.dot(rows, wo[:, 256 * c : 256 * c + 256], preferred_element_type=F32)
        x6[:, 2 * c, :] = part[:, :128]
        x6[:, 2 * c + 1, :] = part[:, 128:]
    for i, offset in enumerate(OUTPUT_OFFSETS):
        to = head_peer(offset)
        row = [x6[slot_smem[0, to * 4 + k]] for k in range(4)]
        s6[i, :16] = jnp.concatenate(row[:2], axis=0).astype(BF16)
        s6[i, 16:] = jnp.concatenate(row[2:], axis=0).astype(BF16)
        if i < 15:
            head_send(s6.at[i], r6.at[i], 6, recv_sem.at[6 if i < FAR_OUTPUTS else 7], offset)

    wait_bytes(r1, send_sem.at[0])
    wait_bytes(rkv, send_sem.at[1])
    for copy in given:
        copy.wait_send()
    for buf, phase in ((r4, 2), (rt4, 3), (r4, 4)):
        wait_bytes(buf.at[pl.ds(0, 7)], send_sem.at[phase])

        @pl.when(core == 1)
        def _(buf=buf, phase=phase):
            wait_bytes(buf.at[0], send_sem.at[phase])

    wait_bytes(r5, send_sem.at[5])

    mixed = s6[15].astype(F32)
    wait_bytes(r6.at[pl.ds(FAR_OUTPUTS, 15 - FAR_OUTPUTS)], recv_sem.at[7])
    for i in range(FAR_OUTPUTS, 15):
        mixed = mixed + r6[i].astype(F32)
    wait_bytes(r6.at[pl.ds(0, FAR_OUTPUTS)], recv_sem.at[6])
    for i in range(FAR_OUTPUTS):
        mixed = mixed + r6[i].astype(F32)
    out_ref[...] = mixed
    wait_bytes(r6, send_sem.at[6])


def local(hidden_in, w_query, w_key, w_value, w_out, k_cache, v_cache, cache_len, slot_of):
    hbm = pl.BlockSpec(memory_space=pl.ANY)
    vmem = pl.BlockSpec(memory_space=pltpu.VMEM)
    return pl.pallas_call(
        kernel,
        out_shape=pltpu.VMEM((32, 128), F32),
        in_specs=[hbm] * 9,
        out_specs=vmem,
        scratch_shapes=[
            pltpu.VMEM((1, 64), jnp.int32),
            pltpu.VMEM((1, 64), jnp.int32),
            pltpu.SMEM((1, 64), jnp.int32),
            pltpu.VMEM((64, 1024), BF16),
            pltpu.VMEM((1024, 1024), BF16),
            pltpu.VMEM((128, 1024), BF16),
            pltpu.VMEM((1024, 1024), BF16),
            pltpu.VMEM((4, 2, 4, 384, 128), BF16),
            pltpu.VMEM((4, 2, 4, 384, 128), BF16),
            pltpu.VMEM((512, 128), F32),
            pltpu.VMEM((15, 32, 128), F32),
            pltpu.VMEM((16, 4, 128), F32),
            pltpu.VMEM((15, 4, 128), F32),
            pltpu.VMEM((2, 4, 128), F32),
            pltpu.VMEM((32, 128), BF16),
            pltpu.VMEM((4, 2, 32, 128), BF16),
            pltpu.VMEM((4, 2, 32, 128), BF16),
            pltpu.VMEM((8, 32, 128), BF16),
            pltpu.VMEM((4, 2, 1, 128), F32),
            pltpu.VMEM((8, 1, 128), F32),
            pltpu.VMEM((32, 128), BF16),
            pltpu.VMEM((15, 32, 128), BF16),
            pltpu.VMEM((512, 128), F32),
            pltpu.VMEM((64, 8, 128), F32),
            pltpu.VMEM((16, 32, 128), BF16),
            pltpu.VMEM((15, 32, 128), BF16),
            pltpu.SemaphoreType.DMA((11,)),
            pltpu.SemaphoreType.DMA((7,)),
            pltpu.SemaphoreType.DMA((9,)),
            pltpu.SemaphoreType.DMA((4,)),
            pltpu.SemaphoreType.DMA((2,)),
            pltpu.SemaphoreType.DMA((3, 8)),
        ],
        compiler_params=pltpu.CompilerParams(
            collective_id=0, has_side_effects=True, vmem_limit_bytes=63 * 1024 * 1024
        ),
    )(
        hidden_in, w_query, w_key.T, w_value.T, w_out, k_cache, v_cache,
        cache_len.reshape(1, 64), slot_of.reshape(1, 64),
    ).reshape(4, 1024)


def solution(mesh):
    in_specs = (
        P(None, "pool"),
        P("pool", "head"),
        P("pool", "head"),
        P("pool", "head"),
        P("head", "pool"),
        P("pool", "head", None),
        P("pool", "head", None),
        P(),
        P(),
    )
    out_specs = P("head", "pool")
    return jax.shard_map(local, mesh=mesh, in_specs=in_specs, out_specs=out_specs, check_vma=False)
```

```python
import math

import jax
import jax.numpy as jnp
from jax import lax
from jax.experimental import pallas as pl
from jax.experimental.pallas import tpu as pltpu
from jax.sharding import PartitionSpec as P

QH = 128
KVH = 8
HD = 128
THETA = 500000.0
NEGATIVE = -1e30
MESH = pl.DeviceIdType.MESH
F32 = jnp.float32
BF16 = jnp.bfloat16
ACROSS = (((1,), (1,)), ((), ()))

POOL_OFFSETS = sorted(
    [(dy, dx) for dy in range(4) for dx in range(4) if (dy, dx) != (0, 0)],
    key=lambda o: -(min(o[0], 4 - o[0]) + min(o[1], 4 - o[1])),
)
FAR_ROWS = 5
HEAD_OFFSETS = sorted(
    [(dz, dc) for dz in range(8) for dc in range(2) if (dz, dc) != (0, 0)],
    key=lambda o: -(min(o[0], 8 - o[0]) + 0.5 * o[1]),
)
OUTPUT_OFFSETS = sorted(
    HEAD_OFFSETS, key=lambda o: (min(o[0], 8 - o[0]) < 3, -o[1], -min(o[0], 8 - o[0]))
) + [(0, 0)]
FAR_OUTPUTS = 6

BATCHES = ((0,), (3,), (2,), (1,))
CHIP_OFFSETS = (3, 5, 4, 1, 7, 2, 6, 0)


def group_slot(dz):
    return ((8 - dz) % 8 - dz % 2) // 2


def kernel(
    hid_hbm, wq_hbm, wk_hbm, wv_hbm, wo_hbm, k_hbm, v_hbm, len_hbm, slot_hbm, out_ref,
    len_ref, slot_ref, slot_smem, hid, wq, wkv, wo, kc, vc,
    s1, r1, skv, rkv, swap, s2, r2, s4, r4, st4, rt4, s5, r5, x5, x6, s6, r6,
    load_sem, send_sem, recv_sem, query_sem, swap_sem, cache_sem,
):
    head = lax.axis_index("head")
    pool = lax.axis_index("pool")
    z, core = head // 2, head % 2
    py, px = pool // 4, pool % 4

    def pool_peer(offset):
        return lax.rem(py + offset[0], 4) * 4 + lax.rem(px + offset[1], 4)

    def head_peer(offset):
        return lax.rem(z + offset[0], 8) * 2 + lax.rem(core + offset[1], 2)

    def pool_send(src, dst, phase, offset):
        pltpu.make_async_remote_copy(
            src, dst, send_sem.at[phase], recv_sem.at[phase],
            device_id=(head, pool_peer(offset)), device_id_type=MESH,
        ).start()

    def head_send(src, dst, phase, receive, offset):
        pltpu.make_async_remote_copy(
            src, dst, send_sem.at[phase], receive,
            device_id=(head_peer(offset), pool), device_id_type=MESH,
        ).start()

    def wait_bytes(view, sem):
        pltpu.make_async_copy(view, view, sem).wait()

    loads = [
        pltpu.make_async_copy(slot_hbm, slot_ref, load_sem.at[0]),
        pltpu.make_async_copy(hid_hbm, hid, load_sem.at[1]),
    ]
    for c in range(2):
        cols = pl.ds(512 * c, 512)
        loads.append(pltpu.make_async_copy(wq_hbm.at[:, cols], wq.at[:, cols], load_sem.at[2 + c]))
    later = [
        pltpu.make_async_copy(wk_hbm, wkv.at[pl.ds(0, 64)], load_sem.at[6]),
        pltpu.make_async_copy(wv_hbm, wkv.at[pl.ds(64, 64)], load_sem.at[7]),
        pltpu.make_async_copy(len_hbm, len_ref, load_sem.at[8]),
        pltpu.make_async_copy(slot_hbm, slot_smem, load_sem.at[9]),
    ]
    last = pltpu.make_async_copy(wo_hbm, wo, load_sem.at[10])

    def group_lanes(owner, i):
        return pl.ds(pl.multiple_of(lax.rem(z + owner + 2 * i, 8) * 128, 128), 128)

    kept, given = [], []
    for n, (source, cache) in enumerate(((k_hbm, kc), (v_hbm, vc))):
        for i in range(4):
            kept.append(
                pltpu.make_async_copy(
                    source.at[:, :, group_lanes(core, i)], cache.at[i, core], cache_sem.at[0, 4 * n + i]
                )
            )
            given.append(
                pltpu.make_async_remote_copy(
                    source.at[:, :, group_lanes(1 - core, i)], cache.at[i, core],
                    cache_sem.at[1, 4 * n + i], cache_sem.at[2, 4 * n + i],
                    device_id=(z * 2 + 1 - core, pool), device_id_type=MESH,
                )
            )
    barrier = pltpu.get_barrier_semaphore()
    for offset in POOL_OFFSETS:
        pl.semaphore_signal(barrier, inc=1, device_id=(head, pool_peer(offset)), device_id_type=MESH)
    for copy in loads:
        copy.start()
    for offset in HEAD_OFFSETS:
        pl.semaphore_signal(barrier, inc=1, device_id=(head_peer(offset), pool), device_id_type=MESH)

    loads[0].wait()
    slot_row = slot_ref[...]
    to_slot = (lax.broadcasted_iota(jnp.int32, (64, 64), 0) == slot_row).astype(BF16)
    loads[1].wait()
    hidden = jnp.dot(to_slot, hid[...], preferred_element_type=F32).astype(BF16)
    for c in range(2):
        loads[2 + c].wait()
        if c == 1:
            for copy in later + kept + [last]:
                copy.start()
        part = jnp.dot(hidden, wq[:, 512 * c : 512 * c + 512], preferred_element_type=F32)
        for j in range(4):
            s1[pl.ds(4 * c + j, 64, stride=8), :] = part[:, 128 * j : 128 * j + 128]
    pl.semaphore_wait(barrier, 30)
    for i, offset in enumerate(POOL_OFFSETS):
        rows = pl.ds(pl.multiple_of(32 * pool_peer(offset), 32), 32)
        pool_send(s1.at[rows], r1.at[i], 0, offset)
    for copy in given[:4]:
        copy.start()

    later[0].wait()
    later[1].wait()
    key_value = lax.dot_general(hidden, wkv[...], ACROSS, preferred_element_type=F32)
    for p in range(16):
        skv[p] = key_value[4 * p : 4 * p + 4]
    for copy in given[4:]:
        copy.start()

    later[2].wait()
    lane = lax.broadcasted_iota(jnp.int32, (8, 128), 1)
    inverse = jnp.ones((8, 128), F32)
    for bit in range(6):
        step = THETA ** (-2.0 * 2**bit / HD)
        inverse = jnp.where((lane & (1 << bit)) != 0, inverse * step, inverse)
    mine = pool * 4 + lax.broadcasted_iota(jnp.int32, (8, 64), 0) % 4
    lengths = jnp.sum(jnp.where(mine == slot_row, len_ref[...].astype(F32), 0.0), axis=1, keepdims=True)
    angle = lengths * inverse
    cosine = jnp.cos(angle)
    sine = jnp.where(lane < 64, -jnp.sin(angle), jnp.sin(angle))

    def rotate(x, rows):
        return x * cosine[rows] + pltpu.roll(x, 64, 1) * sine[rows]

    wait_bytes(r1, recv_sem.at[0])
    total = s1[pl.ds(pl.multiple_of(32 * pool, 32), 32), :]
    for i in range(15):
        total = total + r1[i]

    query = jnp.concatenate(
        [rotate(total[8 * s : 8 * s + 8], slice(s, s + 1)) for s in range(4)], axis=0
    ).astype(BF16)
    s2[...] = query
    for dz in CHIP_OFFSETS[:-1]:
        i = group_slot(dz)
        pltpu.make_async_remote_copy(
            s2, r2.at[i, core], send_sem.at[2], query_sem.at[i],
            device_id=(lax.rem(z + dz, 8) * 2 + dz % 2, pool), device_id_type=MESH,
        ).start()

    @pl.when(core == 0)
    def _():
        pltpu.make_async_copy(s2, r2.at[0, 0], query_sem.at[0]).start()

    @pl.when(core == 1)
    def _():
        head_send(s2, r2.at[0, 1], 2, query_sem.at[0], (0, 1))

    for i, offset in enumerate(POOL_OFFSETS):
        pool_send(skv.at[pool_peer(offset)], rkv.at[i], 1, offset)

    scale = 1.0 / math.sqrt(HD)
    place = (z * 768 + lax.broadcasted_iota(jnp.int32, (1, 768), 1)).astype(F32)
    valid = [jnp.broadcast_to(place < lengths[s : s + 1, :], (16, 768)) for s in range(4)]
    row32 = lax.broadcasted_iota(jnp.int32, (32, 128), 0)
    lane32 = lax.broadcasted_iota(jnp.int32, (32, 128), 1)
    for batch in BATCHES:
        if batch == BATCHES[-1]:
            wait_bytes(rkv, recv_sem.at[1])
            here = skv[pool]
            for i in range(15):
                here = here + rkv[i]
            swap[0] = here
            swap_copy = pltpu.make_async_remote_copy(
                swap.at[0], swap.at[1], swap_sem.at[0], swap_sem.at[1],
                device_id=(z * 2 + 1 - core, pool), device_id_type=MESH,
            )
            swap_copy.start()
        for i in batch:
            wait_bytes(r2.at[i], query_sem.at[i])
            for n in (i, 4 + i):
                kept[n].wait()
                given[n].wait_recv()
        pairs = [(i, s) for i in batch for s in range(4)]
        arrived = {i: r2[i].astype(F32).reshape(2, 4, 8, 128) for i in batch}
        queries = [arrived[i][:, s].reshape(16, 128).astype(BF16) for i, s in pairs]
        scores = [
            jnp.concatenate(
                [lax.dot_general(q, kc[i, c, s], ACROSS, preferred_element_type=F32) for c in range(2)], axis=1
            ) * scale
            for q, (i, s) in zip(queries, pairs)
        ]
        tops = [
            jnp.max(jnp.where(valid[s], x, NEGATIVE), axis=1, keepdims=True)
            for x, (_, s) in zip(scores, pairs)
        ]
        weights = [
            jnp.where(valid[s], jnp.exp(x - top), 0.0) for x, top, (_, s) in zip(scores, tops, pairs)
        ]
        bottoms = [jnp.sum(x, axis=1, keepdims=True) for x in weights]
        weights = [x.astype(BF16) for x in weights]
        sums = [
            jnp.dot(x[:, :384], vc[i, 0, s], preferred_element_type=F32)
            + jnp.dot(x[:, 384:], vc[i, 1, s], preferred_element_type=F32)
            for x, (i, s) in zip(weights, pairs)
        ]
        for n, i in enumerate(batch):
            mine = slice(4 * n, 4 * n + 4)
            for c in range(2):
                half = slice(8 * c, 8 * c + 8)
                top = jnp.concatenate([x[half] for x in tops[mine]], axis=0)
                bottom = jnp.concatenate([x[half] for x in bottoms[mine]], axis=0)
                row = jnp.where(row32 == lane32, top, 0.0) + jnp.where(row32 + 32 == lane32, bottom, 0.0)
                st4[i, c] = jnp.sum(row, axis=0, keepdims=True)
                s4[i, c] = jnp.concatenate([x[half] for x in sums[mine]], axis=0).astype(BF16)
        for i in batch:
            chip = lax.rem(z + core + 2 * i, 8)
            slot = lax.rem(8 - core - 2 * i + 8, 8)
            for c in range(2):
                remote = [
                    pltpu.make_async_remote_copy(
                        src.at[i, c], dst.at[slot], send_sem.at[phase], recv_sem.at[phase],
                        device_id=(chip * 2 + c, pool), device_id_type=MESH,
                    )
                    for src, dst, phase in ((st4, rt4, 3), (s4, r4, 4))
                ]
                if i or c:
                    for copy in remote:
                        copy.start()
                else:

                    @pl.when(core == 1)
                    def _(remote=remote):
                        for copy in remote:
                            copy.start()

                    @pl.when(core == 0)
                    def _():
                        pltpu.make_async_copy(st4.at[0, 0], rt4.at[0], recv_sem.at[3]).start()
                        pltpu.make_async_copy(s4.at[0, 0], r4.at[0], recv_sem.at[4]).start()

    swap_copy.wait()
    there = swap[1]
    lane4 = lax.broadcasted_iota(jnp.int32, (4, 128), 1)
    here_turned, there_turned = pltpu.roll(here, 64, 1), pltpu.roll(there, 64, 1)
    first = core == 0
    key_raw = jnp.where(lane4 < 64, jnp.where(first, here, there), jnp.where(first, there_turned, here_turned))
    value_raw = jnp.where(lane4 < 64, jnp.where(first, here_turned, there_turned), jnp.where(first, there, here))
    key_new = rotate(key_raw, slice(0, 4)).astype(BF16).astype(F32)
    value_new = value_raw.astype(BF16).astype(F32)

    def spread(x):
        return jnp.concatenate([jnp.broadcast_to(x[s : s + 1], (8, 128)) for s in range(4)], axis=0)

    own = jnp.sum(query.astype(F32) * spread(key_new), axis=1, keepdims=True) * scale
    own = jnp.sum(jnp.where(row32 == lane32, own, 0.0), axis=0, keepdims=True)

    wait_bytes(rt4, recv_sem.at[3])
    parts = jnp.concatenate([rt4[i] for i in range(8)], axis=0)
    largest = jnp.maximum(jnp.max(parts, axis=0, keepdims=True), own)
    factor = jnp.exp(parts - largest)
    own_weight = jnp.exp(own - largest)
    denominator = jnp.sum(factor * pltpu.roll(parts, 96, 1), axis=0, keepdims=True) + own_weight
    shares = jnp.concatenate(
        [factor / denominator, own_weight.astype(BF16).astype(F32) / denominator, jnp.zeros((7, 128), F32)], axis=0
    ).T
    attention = shares[:32, 8:9] * spread(value_new)
    wait_bytes(r4, recv_sem.at[4])
    for i in range(8):
        attention = attention + shares[:32, i : i + 1] * r4[i].astype(F32)
    attention = attention.astype(BF16)

    s5[...] = attention
    for i, offset in enumerate(POOL_OFFSETS):
        pltpu.make_async_remote_copy(
            s5, r5.at[i], send_sem.at[5], recv_sem.at[5 if i < FAR_ROWS else 8],
            device_id=(head, pool_peer(offset)), device_id_type=MESH,
        ).start()
    later[3].wait()
    last.wait()

    def place_rows(source, block):
        x5[pl.ds(pl.multiple_of(source * 32, 32), 32), :] = block.astype(F32)

    place_rows(pool, s5[...])
    wait_bytes(r5.at[pl.ds(FAR_ROWS, 15 - FAR_ROWS)], recv_sem.at[8])
    for i in range(FAR_ROWS, 15):
        place_rows(pool_peer([4 - o for o in POOL_OFFSETS[i]]), r5[i])
    wait_bytes(r5.at[pl.ds(0, FAR_ROWS)], recv_sem.at[5])
    for i in range(FAR_ROWS):
        place_rows(pool_peer([4 - o for o in POOL_OFFSETS[i]]), r5[i])
    rows = jnp.concatenate([x5[pl.ds(j, 64, stride=8), :].astype(BF16) for j in range(8)], axis=1)

    part = jnp.dot(rows, wo[...], preferred_element_type=F32)
    for j in range(8):
        x6[:, j, :] = part[:, 128 * j : 128 * j + 128]
    for i, offset in enumerate(OUTPUT_OFFSETS):
        to = head_peer(offset)
        row = [x6[slot_smem[0, to * 4 + k]] for k in range(4)]
        s6[i, :16] = jnp.concatenate(row[:2], axis=0).astype(BF16)
        s6[i, 16:] = jnp.concatenate(row[2:], axis=0).astype(BF16)
        if i < 15:
            head_send(s6.at[i], r6.at[i], 6, recv_sem.at[6 if i < FAR_OUTPUTS else 7], offset)

    wait_bytes(r1, send_sem.at[0])
    wait_bytes(rkv, send_sem.at[1])
    for copy in given:
        copy.wait_send()
    for buf, phase in ((r4, 2), (rt4, 3), (r4, 4)):
        wait_bytes(buf.at[pl.ds(0, 7)], send_sem.at[phase])

        @pl.when(core == 1)
        def _(buf=buf, phase=phase):
            wait_bytes(buf.at[0], send_sem.at[phase])

    wait_bytes(r5, send_sem.at[5])

    mixed = s6[15].astype(F32)
    wait_bytes(r6.at[pl.ds(FAR_OUTPUTS, 15 - FAR_OUTPUTS)], recv_sem.at[7])
    for i in range(FAR_OUTPUTS, 15):
        mixed = mixed + r6[i].astype(F32)
    wait_bytes(r6.at[pl.ds(0, FAR_OUTPUTS)], recv_sem.at[6])
    for i in range(FAR_OUTPUTS):
        mixed = mixed + r6[i].astype(F32)
    out_ref[...] = mixed
    wait_bytes(r6, send_sem.at[6])


def local(hidden_in, w_query, w_key, w_value, w_out, k_cache, v_cache, cache_len, slot_of):
    hbm = pl.BlockSpec(memory_space=pl.ANY)
    vmem = pl.BlockSpec(memory_space=pltpu.VMEM)
    return pl.pallas_call(
        kernel,
        out_shape=pltpu.VMEM((32, 128), F32),
        in_specs=[hbm] * 9,
        out_specs=vmem,
        scratch_shapes=[
            pltpu.VMEM((1, 64), jnp.int32),
            pltpu.VMEM((1, 64), jnp.int32),
            pltpu.SMEM((1, 64), jnp.int32),
            pltpu.VMEM((64, 1024), BF16),
            pltpu.VMEM((1024, 1024), BF16),
            pltpu.VMEM((128, 1024), BF16),
            pltpu.VMEM((1024, 1024), BF16),
            pltpu.VMEM((4, 2, 4, 384, 128), BF16),
            pltpu.VMEM((4, 2, 4, 384, 128), BF16),
            pltpu.VMEM((512, 128), F32),
            pltpu.VMEM((15, 32, 128), F32),
            pltpu.VMEM((16, 4, 128), F32),
            pltpu.VMEM((15, 4, 128), F32),
            pltpu.VMEM((2, 4, 128), F32),
            pltpu.VMEM((32, 128), BF16),
            pltpu.VMEM((4, 2, 32, 128), BF16),
            pltpu.VMEM((4, 2, 32, 128), BF16),
            pltpu.VMEM((8, 32, 128), BF16),
            pltpu.VMEM((4, 2, 1, 128), F32),
            pltpu.VMEM((8, 1, 128), F32),
            pltpu.VMEM((32, 128), BF16),
            pltpu.VMEM((15, 32, 128), BF16),
            pltpu.VMEM((512, 128), F32),
            pltpu.VMEM((64, 8, 128), F32),
            pltpu.VMEM((16, 32, 128), BF16),
            pltpu.VMEM((15, 32, 128), BF16),
            pltpu.SemaphoreType.DMA((11,)),
            pltpu.SemaphoreType.DMA((7,)),
            pltpu.SemaphoreType.DMA((9,)),
            pltpu.SemaphoreType.DMA((4,)),
            pltpu.SemaphoreType.DMA((2,)),
            pltpu.SemaphoreType.DMA((3, 8)),
        ],
        compiler_params=pltpu.CompilerParams(
            collective_id=0, has_side_effects=True, vmem_limit_bytes=63 * 1024 * 1024
        ),
    )(
        hidden_in, w_query, w_key.T, w_value.T, w_out, k_cache, v_cache,
        cache_len.reshape(1, 64), slot_of.reshape(1, 64),
    ).reshape(4, 1024)


def solution(mesh):
    in_specs = (
        P(None, "pool"),
        P("pool", "head"),
        P("pool", "head"),
        P("pool", "head"),
        P("head", "pool"),
        P("pool", "head", None),
        P("pool", "head", None),
        P(),
        P(),
    )
    out_specs = P("head", "pool")
    return jax.shard_map(local, mesh=mesh, in_specs=in_specs, out_specs=out_specs, check_vma=False)
```

```python
import math

import jax
import jax.numpy as jnp
from jax import lax
from jax.experimental import pallas as pl
from jax.experimental.pallas import tpu as pltpu
from jax.sharding import PartitionSpec as P

QH = 128
KVH = 8
HD = 128
THETA = 500000.0
NEGATIVE = -1e30
MESH = pl.DeviceIdType.MESH
F32 = jnp.float32
BF16 = jnp.bfloat16
ACROSS = (((1,), (1,)), ((), ()))

POOL_OFFSETS = sorted(
    [(dy, dx) for dy in range(4) for dx in range(4) if (dy, dx) != (0, 0)],
    key=lambda o: -(min(o[0], 4 - o[0]) + min(o[1], 4 - o[1])),
)
FAR_ROWS = 5
HEAD_OFFSETS = sorted(
    [(dz, dc) for dz in range(8) for dc in range(2) if (dz, dc) != (0, 0)],
    key=lambda o: -(min(o[0], 8 - o[0]) + 0.5 * o[1]),
)
OUTPUT_OFFSETS = sorted(
    HEAD_OFFSETS, key=lambda o: (min(o[0], 8 - o[0]) < 3, -o[1], -min(o[0], 8 - o[0]))
) + [(0, 0)]
FAR_OUTPUTS = 6

BATCHES = ((0,), (3,), (2,), (1,))
CHIP_OFFSETS = (4, 1, 7, 2, 6, 3, 5, 0)


def group_slot(dz):
    return ((8 - dz) % 8 - dz % 2) // 2


def kernel(
    hid_hbm, wq_hbm, wk_hbm, wv_hbm, wo_hbm, k_hbm, v_hbm, len_hbm, slot_hbm, out_ref,
    len_ref, slot_ref, slot_smem, hid, wq, wkv, wo, kc, vc,
    s1, r1, skv, rkv, swap, s2, r2, s4, r4, st4, rt4, s5, r5, x5, x6, s6, r6,
    load_sem, send_sem, recv_sem, query_sem, swap_sem, cache_sem,
):
    head = lax.axis_index("head")
    pool = lax.axis_index("pool")
    z, core = head // 2, head % 2
    py, px = pool // 4, pool % 4

    def pool_peer(offset):
        return lax.rem(py + offset[0], 4) * 4 + lax.rem(px + offset[1], 4)

    def head_peer(offset):
        return lax.rem(z + offset[0], 8) * 2 + lax.rem(core + offset[1], 2)

    def pool_send(src, dst, phase, offset):
        pltpu.make_async_remote_copy(
            src, dst, send_sem.at[phase], recv_sem.at[phase],
            device_id=(head, pool_peer(offset)), device_id_type=MESH,
        ).start()

    def head_send(src, dst, phase, receive, offset):
        pltpu.make_async_remote_copy(
            src, dst, send_sem.at[phase], receive,
            device_id=(head_peer(offset), pool), device_id_type=MESH,
        ).start()

    def wait_bytes(view, sem):
        pltpu.make_async_copy(view, view, sem).wait()

    loads = [
        pltpu.make_async_copy(slot_hbm, slot_ref, load_sem.at[0]),
        pltpu.make_async_copy(hid_hbm, hid, load_sem.at[1]),
    ]
    for c in range(2):
        cols = pl.ds(512 * c, 512)
        loads.append(pltpu.make_async_copy(wq_hbm.at[:, cols], wq.at[:, cols], load_sem.at[2 + c]))
    later = [
        pltpu.make_async_copy(wk_hbm, wkv.at[pl.ds(0, 64)], load_sem.at[6]),
        pltpu.make_async_copy(wv_hbm, wkv.at[pl.ds(64, 64)], load_sem.at[7]),
        pltpu.make_async_copy(len_hbm, len_ref, load_sem.at[8]),
        pltpu.make_async_copy(slot_hbm, slot_smem, load_sem.at[9]),
    ]
    last = pltpu.make_async_copy(wo_hbm, wo, load_sem.at[10])

    def group_lanes(owner, i):
        return pl.ds(pl.multiple_of(lax.rem(z + owner + 2 * i, 8) * 128, 128), 128)

    kept, given = [], []
    for n, (source, cache) in enumerate(((k_hbm, kc), (v_hbm, vc))):
        for i in range(4):
            kept.append(
                pltpu.make_async_copy(
                    source.at[:, :, group_lanes(core, i)], cache.at[i, core], cache_sem.at[0, 4 * n + i]
                )
            )
            given.append(
                pltpu.make_async_remote_copy(
                    source.at[:, :, group_lanes(1 - core, i)], cache.at[i, core],
                    cache_sem.at[1, 4 * n + i], cache_sem.at[2, 4 * n + i],
                    device_id=(z * 2 + 1 - core, pool), device_id_type=MESH,
                )
            )
    barrier = pltpu.get_barrier_semaphore()
    for offset in POOL_OFFSETS:
        pl.semaphore_signal(barrier, inc=1, device_id=(head, pool_peer(offset)), device_id_type=MESH)
    for copy in loads:
        copy.start()
    for offset in HEAD_OFFSETS:
        pl.semaphore_signal(barrier, inc=1, device_id=(head_peer(offset), pool), device_id_type=MESH)

    loads[0].wait()
    slot_row = slot_ref[...]
    to_slot = (lax.broadcasted_iota(jnp.int32, (64, 64), 0) == slot_row).astype(BF16)
    loads[1].wait()
    hidden = jnp.dot(to_slot, hid[...], preferred_element_type=F32).astype(BF16)
    for c in range(2):
        loads[2 + c].wait()
        if c == 1:
            for copy in later + kept + [last]:
                copy.start()
        part = jnp.dot(hidden, wq[:, 512 * c : 512 * c + 512], preferred_element_type=F32)
        for j in range(4):
            s1[pl.ds(4 * c + j, 64, stride=8), :] = part[:, 128 * j : 128 * j + 128]
    pl.semaphore_wait(barrier, 30)
    for i, offset in enumerate(POOL_OFFSETS):
        rows = pl.ds(pl.multiple_of(32 * pool_peer(offset), 32), 32)
        pool_send(s1.at[rows], r1.at[i], 0, offset)
    for copy in given[:4]:
        copy.start()

    later[0].wait()
    later[1].wait()
    key_value = lax.dot_general(hidden, wkv[...], ACROSS, preferred_element_type=F32)
    for p in range(16):
        skv[p] = key_value[4 * p : 4 * p + 4]
    for copy in given[4:]:
        copy.start()

    later[2].wait()
    lane = lax.broadcasted_iota(jnp.int32, (8, 128), 1)
    inverse = jnp.ones((8, 128), F32)
    for bit in range(6):
        step = THETA ** (-2.0 * 2**bit / HD)
        inverse = jnp.where((lane & (1 << bit)) != 0, inverse * step, inverse)
    mine = pool * 4 + lax.broadcasted_iota(jnp.int32, (8, 64), 0) % 4
    lengths = jnp.sum(jnp.where(mine == slot_row, len_ref[...].astype(F32), 0.0), axis=1, keepdims=True)
    angle = lengths * inverse
    cosine = jnp.cos(angle)
    sine = jnp.where(lane < 64, -jnp.sin(angle), jnp.sin(angle))

    def rotate(x, rows):
        return x * cosine[rows] + pltpu.roll(x, 64, 1) * sine[rows]

    wait_bytes(r1, recv_sem.at[0])
    total = s1[pl.ds(pl.multiple_of(32 * pool, 32), 32), :]
    for i in range(15):
        total = total + r1[i]

    query = jnp.concatenate(
        [rotate(total[8 * s : 8 * s + 8], slice(s, s + 1)) for s in range(4)], axis=0
    ).astype(BF16)
    s2[...] = query
    for dz in CHIP_OFFSETS[:-1]:
        i = group_slot(dz)
        pltpu.make_async_remote_copy(
            s2, r2.at[i, core], send_sem.at[2], query_sem.at[i],
            device_id=(lax.rem(z + dz, 8) * 2 + dz % 2, pool), device_id_type=MESH,
        ).start()

    @pl.when(core == 0)
    def _():
        pltpu.make_async_copy(s2, r2.at[0, 0], query_sem.at[0]).start()

    @pl.when(core == 1)
    def _():
        head_send(s2, r2.at[0, 1], 2, query_sem.at[0], (0, 1))

    for i, offset in enumerate(POOL_OFFSETS):
        pool_send(skv.at[pool_peer(offset)], rkv.at[i], 1, offset)

    scale = 1.0 / math.sqrt(HD)
    place = (z * 768 + lax.broadcasted_iota(jnp.int32, (1, 768), 1)).astype(F32)
    valid = [jnp.broadcast_to(place < lengths[s : s + 1, :], (16, 768)) for s in range(4)]
    row32 = lax.broadcasted_iota(jnp.int32, (32, 128), 0)
    lane32 = lax.broadcasted_iota(jnp.int32, (32, 128), 1)
    for batch in BATCHES:
        if batch == BATCHES[-1]:
            wait_bytes(rkv, recv_sem.at[1])
            here = skv[pool]
            for i in range(15):
                here = here + rkv[i]
            swap[0] = here
            swap_copy = pltpu.make_async_remote_copy(
                swap.at[0], swap.at[1], swap_sem.at[0], swap_sem.at[1],
                device_id=(z * 2 + 1 - core, pool), device_id_type=MESH,
            )
            swap_copy.start()
        for i in batch:
            wait_bytes(r2.at[i], query_sem.at[i])
            for n in (i, 4 + i):
                kept[n].wait()
                given[n].wait_recv()
        pairs = [(i, s) for i in batch for s in range(4)]
        arrived = {i: r2[i].astype(F32).reshape(2, 4, 8, 128) for i in batch}
        queries = [arrived[i][:, s].reshape(16, 128).astype(BF16) for i, s in pairs]
        scores = []
        blank = jnp.zeros((16, 128), BF16)
        for n in range(0, len(pairs), 2):
            i, s = pairs[n]
            both = jnp.concatenate(
                [
                    jnp.concatenate([queries[n], blank], axis=1),
                    jnp.concatenate([blank, queries[n + 1]], axis=1),
                ],
                axis=0,
            )
            found = jnp.concatenate(
                [
                    lax.dot_general(
                        both, jnp.concatenate([kc[i, c, s], kc[i, c, s + 1]], axis=1), ACROSS,
                        preferred_element_type=F32,
                    )
                    for c in range(2)
                ],
                axis=1,
            ) * scale
            scores += [found[:16], found[16:]]
        tops = [
            jnp.max(jnp.where(valid[s], x, NEGATIVE), axis=1, keepdims=True)
            for x, (_, s) in zip(scores, pairs)
        ]
        weights = [
            jnp.where(valid[s], jnp.exp(x - top), 0.0) for x, top, (_, s) in zip(scores, tops, pairs)
        ]
        bottoms = [jnp.sum(x, axis=1, keepdims=True) for x in weights]
        weights = [x.astype(BF16) for x in weights]
        sums = [
            jnp.dot(x[:, :384], vc[i, 0, s], preferred_element_type=F32)
            + jnp.dot(x[:, 384:], vc[i, 1, s], preferred_element_type=F32)
            for x, (i, s) in zip(weights, pairs)
        ]
        for n, i in enumerate(batch):
            mine = slice(4 * n, 4 * n + 4)
            for c in range(2):
                half = slice(8 * c, 8 * c + 8)
                top = jnp.concatenate([x[half] for x in tops[mine]], axis=0)
                bottom = jnp.concatenate([x[half] for x in bottoms[mine]], axis=0)
                row = jnp.where(row32 == lane32, top, 0.0) + jnp.where(row32 + 32 == lane32, bottom, 0.0)
                st4[i, c] = jnp.sum(row, axis=0, keepdims=True)
                s4[i, c] = jnp.concatenate([x[half] for x in sums[mine]], axis=0).astype(BF16)
        for i in batch:
            chip = lax.rem(z + core + 2 * i, 8)
            slot = lax.rem(8 - core - 2 * i + 8, 8)
            for c in range(2):
                remote = [
                    pltpu.make_async_remote_copy(
                        src.at[i, c], dst.at[slot], send_sem.at[phase], recv_sem.at[phase],
                        device_id=(chip * 2 + c, pool), device_id_type=MESH,
                    )
                    for src, dst, phase in ((st4, rt4, 3), (s4, r4, 4))
                ]
                if i or c:
                    for copy in remote:
                        copy.start()
                else:

                    @pl.when(core == 1)
                    def _(remote=remote):
                        for copy in remote:
                            copy.start()

                    @pl.when(core == 0)
                    def _():
                        pltpu.make_async_copy(st4.at[0, 0], rt4.at[0], recv_sem.at[3]).start()
                        pltpu.make_async_copy(s4.at[0, 0], r4.at[0], recv_sem.at[4]).start()

    swap_copy.wait()
    there = swap[1]
    lane4 = lax.broadcasted_iota(jnp.int32, (4, 128), 1)
    here_turned, there_turned = pltpu.roll(here, 64, 1), pltpu.roll(there, 64, 1)
    first = core == 0
    key_raw = jnp.where(lane4 < 64, jnp.where(first, here, there), jnp.where(first, there_turned, here_turned))
    value_raw = jnp.where(lane4 < 64, jnp.where(first, here_turned, there_turned), jnp.where(first, there, here))
    key_new = rotate(key_raw, slice(0, 4)).astype(BF16).astype(F32)
    value_new = value_raw.astype(BF16).astype(F32)

    def spread(x):
        return jnp.concatenate([jnp.broadcast_to(x[s : s + 1], (8, 128)) for s in range(4)], axis=0)

    own = jnp.sum(query.astype(F32) * spread(key_new), axis=1, keepdims=True) * scale
    own = jnp.sum(jnp.where(row32 == lane32, own, 0.0), axis=0, keepdims=True)

    wait_bytes(rt4, recv_sem.at[3])
    parts = jnp.concatenate([rt4[i] for i in range(8)], axis=0)
    largest = jnp.maximum(jnp.max(parts, axis=0, keepdims=True), own)
    factor = jnp.exp(parts - largest)
    own_weight = jnp.exp(own - largest)
    denominator = jnp.sum(factor * pltpu.roll(parts, 96, 1), axis=0, keepdims=True) + own_weight
    shares = jnp.concatenate(
        [factor / denominator, own_weight.astype(BF16).astype(F32) / denominator, jnp.zeros((7, 128), F32)], axis=0
    ).T
    attention = shares[:32, 8:9] * spread(value_new)
    wait_bytes(r4, recv_sem.at[4])
    for i in range(8):
        attention = attention + shares[:32, i : i + 1] * r4[i].astype(F32)
    attention = attention.astype(BF16)

    s5[...] = attention
    for i, offset in enumerate(POOL_OFFSETS):
        pltpu.make_async_remote_copy(
            s5, r5.at[i], send_sem.at[5], recv_sem.at[5 if i < FAR_ROWS else 8],
            device_id=(head, pool_peer(offset)), device_id_type=MESH,
        ).start()
    later[3].wait()
    last.wait()

    def place_rows(source, block):
        x5[pl.ds(pl.multiple_of(source * 32, 32), 32), :] = block.astype(F32)

    place_rows(pool, s5[...])
    wait_bytes(r5.at[pl.ds(FAR_ROWS, 15 - FAR_ROWS)], recv_sem.at[8])
    for i in range(FAR_ROWS, 15):
        place_rows(pool_peer([4 - o for o in POOL_OFFSETS[i]]), r5[i])
    wait_bytes(r5.at[pl.ds(0, FAR_ROWS)], recv_sem.at[5])
    for i in range(FAR_ROWS):
        place_rows(pool_peer([4 - o for o in POOL_OFFSETS[i]]), r5[i])
    rows = jnp.concatenate([x5[pl.ds(j, 64, stride=8), :].astype(BF16) for j in range(8)], axis=1)

    part = jnp.dot(rows, wo[...], preferred_element_type=F32)
    for j in range(8):
        x6[:, j, :] = part[:, 128 * j : 128 * j + 128]
    for i, offset in enumerate(OUTPUT_OFFSETS):
        to = head_peer(offset)
        row = [x6[slot_smem[0, to * 4 + k]] for k in range(4)]
        s6[i, :16] = jnp.concatenate(row[:2], axis=0).astype(BF16)
        s6[i, 16:] = jnp.concatenate(row[2:], axis=0).astype(BF16)
        if i < 15:
            head_send(s6.at[i], r6.at[i], 6, recv_sem.at[6 if i < FAR_OUTPUTS else 7], offset)

    wait_bytes(r1, send_sem.at[0])
    wait_bytes(rkv, send_sem.at[1])
    for copy in given:
        copy.wait_send()
    for buf, phase in ((r4, 2), (rt4, 3), (r4, 4)):
        wait_bytes(buf.at[pl.ds(0, 7)], send_sem.at[phase])

        @pl.when(core == 1)
        def _(buf=buf, phase=phase):
            wait_bytes(buf.at[0], send_sem.at[phase])

    wait_bytes(r5, send_sem.at[5])

    mixed = s6[15].astype(F32)
    wait_bytes(r6.at[pl.ds(FAR_OUTPUTS, 15 - FAR_OUTPUTS)], recv_sem.at[7])
    for i in range(FAR_OUTPUTS, 15):
        mixed = mixed + r6[i].astype(F32)
    wait_bytes(r6.at[pl.ds(0, FAR_OUTPUTS)], recv_sem.at[6])
    for i in range(FAR_OUTPUTS):
        mixed = mixed + r6[i].astype(F32)
    out_ref[...] = mixed
    wait_bytes(r6, send_sem.at[6])


def local(hidden_in, w_query, w_key, w_value, w_out, k_cache, v_cache, cache_len, slot_of):
    hbm = pl.BlockSpec(memory_space=pl.ANY)
    vmem = pl.BlockSpec(memory_space=pltpu.VMEM)
    return pl.pallas_call(
        kernel,
        out_shape=pltpu.VMEM((32, 128), F32),
        in_specs=[hbm] * 9,
        out_specs=vmem,
        scratch_shapes=[
            pltpu.VMEM((1, 64), jnp.int32),
            pltpu.VMEM((1, 64), jnp.int32),
            pltpu.SMEM((1, 64), jnp.int32),
            pltpu.VMEM((64, 1024), BF16),
            pltpu.VMEM((1024, 1024), BF16),
            pltpu.VMEM((128, 1024), BF16),
            pltpu.VMEM((1024, 1024), BF16),
            pltpu.VMEM((4, 2, 4, 384, 128), BF16),
            pltpu.VMEM((4, 2, 4, 384, 128), BF16),
            pltpu.VMEM((512, 128), F32),
            pltpu.VMEM((15, 32, 128), F32),
            pltpu.VMEM((16, 4, 128), F32),
            pltpu.VMEM((15, 4, 128), F32),
            pltpu.VMEM((2, 4, 128), F32),
            pltpu.VMEM((32, 128), BF16),
            pltpu.VMEM((4, 2, 32, 128), BF16),
            pltpu.VMEM((4, 2, 32, 128), BF16),
            pltpu.VMEM((8, 32, 128), BF16),
            pltpu.VMEM((4, 2, 1, 128), F32),
            pltpu.VMEM((8, 1, 128), F32),
            pltpu.VMEM((32, 128), BF16),
            pltpu.VMEM((15, 32, 128), BF16),
            pltpu.VMEM((512, 128), F32),
            pltpu.VMEM((64, 8, 128), F32),
            pltpu.VMEM((16, 32, 128), BF16),
            pltpu.VMEM((15, 32, 128), BF16),
            pltpu.SemaphoreType.DMA((11,)),
            pltpu.SemaphoreType.DMA((7,)),
            pltpu.SemaphoreType.DMA((9,)),
            pltpu.SemaphoreType.DMA((4,)),
            pltpu.SemaphoreType.DMA((2,)),
            pltpu.SemaphoreType.DMA((3, 8)),
        ],
        compiler_params=pltpu.CompilerParams(
            collective_id=0, has_side_effects=True, vmem_limit_bytes=63 * 1024 * 1024
        ),
    )(
        hidden_in, w_query, w_key.T, w_value.T, w_out, k_cache, v_cache,
        cache_len.reshape(1, 64), slot_of.reshape(1, 64),
    ).reshape(4, 1024)


def solution(mesh):
    in_specs = (
        P(None, "pool"),
        P("pool", "head"),
        P("pool", "head"),
        P("pool", "head"),
        P("head", "pool"),
        P("pool", "head", None),
        P("pool", "head", None),
        P(),
        P(),
    )
    out_specs = P("head", "pool")
    return jax.shard_map(local, mesh=mesh, in_specs=in_specs, out_specs=out_specs, check_vma=False)
```

```python
import math

import jax
import jax.numpy as jnp
from jax import lax
from jax.experimental import pallas as pl
from jax.experimental.pallas import tpu as pltpu
from jax.sharding import PartitionSpec as P

QH = 128
KVH = 8
HD = 128
THETA = 500000.0
NEGATIVE = -1e30
MESH = pl.DeviceIdType.MESH
F32 = jnp.float32
BF16 = jnp.bfloat16
ACROSS = (((1,), (1,)), ((), ()))

POOL_OFFSETS = sorted(
    [(dy, dx) for dy in range(4) for dx in range(4) if (dy, dx) != (0, 0)],
    key=lambda o: -(min(o[0], 4 - o[0]) + min(o[1], 4 - o[1])),
)
FAR_ROWS = 5
HEAD_OFFSETS = sorted(
    [(dz, dc) for dz in range(8) for dc in range(2) if (dz, dc) != (0, 0)],
    key=lambda o: -(min(o[0], 8 - o[0]) + 0.5 * o[1]),
)
OUTPUT_OFFSETS = sorted(
    HEAD_OFFSETS, key=lambda o: (min(o[0], 8 - o[0]) < 3, -o[1], -min(o[0], 8 - o[0]))
) + [(0, 0)]
FAR_OUTPUTS = 6

BATCHES = ((0,), (3,), (2,), (1,))
CHIP_OFFSETS = (4, 1, 7, 2, 6, 3, 5, 0)


def group_slot(dz):
    return ((8 - dz) % 8 - dz % 2) // 2


def kernel(
    hid_hbm, wq_hbm, wk_hbm, wv_hbm, wo_hbm, k_hbm, v_hbm, len_hbm, slot_hbm, out_ref,
    len_ref, slot_ref, slot_smem, hid, wq, wkv, wo, kc, vc,
    s1, r1, skv, rkv, swap, s2, r2, s4, r4, st4, rt4, s5, r5, x5, x6, s6, r6,
    load_sem, send_sem, recv_sem, query_sem, swap_sem, cache_sem,
):
    head = lax.axis_index("head")
    pool = lax.axis_index("pool")
    z, core = head // 2, head % 2
    py, px = pool // 4, pool % 4

    def pool_peer(offset):
        return lax.rem(py + offset[0], 4) * 4 + lax.rem(px + offset[1], 4)

    def head_peer(offset):
        return lax.rem(z + offset[0], 8) * 2 + lax.rem(core + offset[1], 2)

    def pool_send(src, dst, phase, offset):
        pltpu.make_async_remote_copy(
            src, dst, send_sem.at[phase], recv_sem.at[phase],
            device_id=(head, pool_peer(offset)), device_id_type=MESH,
        ).start()

    def head_send(src, dst, phase, receive, offset):
        pltpu.make_async_remote_copy(
            src, dst, send_sem.at[phase], receive,
            device_id=(head_peer(offset), pool), device_id_type=MESH,
        ).start()

    def wait_bytes(view, sem):
        pltpu.make_async_copy(view, view, sem).wait()

    loads = [
        pltpu.make_async_copy(slot_hbm, slot_ref, load_sem.at[0]),
        pltpu.make_async_copy(hid_hbm, hid, load_sem.at[1]),
    ]
    for c in range(2):
        cols = pl.ds(512 * c, 512)
        loads.append(pltpu.make_async_copy(wq_hbm.at[:, cols], wq.at[:, cols], load_sem.at[2 + c]))
    later = [
        pltpu.make_async_copy(wk_hbm, wkv.at[pl.ds(0, 64)], load_sem.at[6]),
        pltpu.make_async_copy(wv_hbm, wkv.at[pl.ds(64, 64)], load_sem.at[7]),
        pltpu.make_async_copy(len_hbm, len_ref, load_sem.at[8]),
        pltpu.make_async_copy(slot_hbm, slot_smem, load_sem.at[9]),
    ]
    last = pltpu.make_async_copy(wo_hbm, wo, load_sem.at[10])

    def group_lanes(owner, i):
        return pl.ds(pl.multiple_of(lax.rem(z + owner + 2 * i, 8) * 128, 128), 128)

    kept, given = [], []
    for n, (source, cache) in enumerate(((k_hbm, kc), (v_hbm, vc))):
        for i in range(4):
            kept.append(
                pltpu.make_async_copy(
                    source.at[:, :, group_lanes(core, i)], cache.at[i, core], cache_sem.at[0, 4 * n + i]
                )
            )
            given.append(
                pltpu.make_async_remote_copy(
                    source.at[:, :, group_lanes(1 - core, i)], cache.at[i, core],
                    cache_sem.at[1, 4 * n + i], cache_sem.at[2, 4 * n + i],
                    device_id=(z * 2 + 1 - core, pool), device_id_type=MESH,
                )
            )
    barrier = pltpu.get_barrier_semaphore()
    for offset in POOL_OFFSETS:
        pl.semaphore_signal(barrier, inc=1, device_id=(head, pool_peer(offset)), device_id_type=MESH)
    for copy in loads:
        copy.start()
    for offset in HEAD_OFFSETS:
        pl.semaphore_signal(barrier, inc=1, device_id=(head_peer(offset), pool), device_id_type=MESH)

    loads[0].wait()
    slot_row = slot_ref[...]
    to_slot = (lax.broadcasted_iota(jnp.int32, (64, 64), 0) == slot_row).astype(BF16)
    loads[1].wait()
    hidden = jnp.dot(to_slot, hid[...], preferred_element_type=F32).astype(BF16)
    for c in range(2):
        loads[2 + c].wait()
        if c == 1:
            for copy in later + kept + [last]:
                copy.start()
        part = jnp.dot(hidden, wq[:, 512 * c : 512 * c + 512], preferred_element_type=F32)
        for j in range(4):
            s1[pl.ds(4 * c + j, 64, stride=8), :] = part[:, 128 * j : 128 * j + 128]
    pl.semaphore_wait(barrier, 30)
    for i, offset in enumerate(POOL_OFFSETS):
        rows = pl.ds(pl.multiple_of(32 * pool_peer(offset), 32), 32)
        pool_send(s1.at[rows], r1.at[i], 0, offset)
    for copy in given[:4]:
        copy.start()

    later[0].wait()
    later[1].wait()
    key_value = lax.dot_general(hidden, wkv[...], ACROSS, preferred_element_type=F32)
    for p in range(16):
        skv[p] = key_value[4 * p : 4 * p + 4]
    for copy in given[4:]:
        copy.start()

    later[2].wait()
    lane = lax.broadcasted_iota(jnp.int32, (8, 128), 1)
    inverse = jnp.ones((8, 128), F32)
    for bit in range(6):
        step = THETA ** (-2.0 * 2**bit / HD)
        inverse = jnp.where((lane & (1 << bit)) != 0, inverse * step, inverse)
    mine = pool * 4 + lax.broadcasted_iota(jnp.int32, (8, 64), 0) % 4
    lengths = jnp.sum(jnp.where(mine == slot_row, len_ref[...].astype(F32), 0.0), axis=1, keepdims=True)
    angle = lengths * inverse
    cosine = jnp.cos(angle)
    sine = jnp.where(lane < 64, -jnp.sin(angle), jnp.sin(angle))

    def rotate(x, rows):
        return x * cosine[rows] + pltpu.roll(x, 64, 1) * sine[rows]

    wait_bytes(r1, recv_sem.at[0])
    total = s1[pl.ds(pl.multiple_of(32 * pool, 32), 32), :]
    for i in range(15):
        total = total + r1[i]

    query = jnp.concatenate(
        [rotate(total[8 * s : 8 * s + 8], slice(s, s + 1)) for s in range(4)], axis=0
    ).astype(BF16)
    s2[...] = query
    for dz in CHIP_OFFSETS[:-1]:
        i = group_slot(dz)
        pltpu.make_async_remote_copy(
            s2, r2.at[i, core], send_sem.at[2], query_sem.at[i],
            device_id=(lax.rem(z + dz, 8) * 2 + dz % 2, pool), device_id_type=MESH,
        ).start()

    @pl.when(core == 0)
    def _():
        pltpu.make_async_copy(s2, r2.at[0, 0], query_sem.at[0]).start()

    @pl.when(core == 1)
    def _():
        head_send(s2, r2.at[0, 1], 2, query_sem.at[0], (0, 1))

    for i, offset in enumerate(POOL_OFFSETS):
        pool_send(skv.at[pool_peer(offset)], rkv.at[i], 1, offset)

    scale = 1.0 / math.sqrt(HD)
    place = (z * 768 + lax.broadcasted_iota(jnp.int32, (1, 768), 1)).astype(F32)
    valid = [jnp.broadcast_to(place < lengths[s : s + 1, :], (16, 768)) for s in range(4)]
    row32 = lax.broadcasted_iota(jnp.int32, (32, 128), 0)
    lane32 = lax.broadcasted_iota(jnp.int32, (32, 128), 1)
    for batch in BATCHES:
        if batch == BATCHES[-1]:
            wait_bytes(rkv, recv_sem.at[1])
            here = skv[pool]
            for i in range(15):
                here = here + rkv[i]
            swap[0] = here
            swap_copy = pltpu.make_async_remote_copy(
                swap.at[0], swap.at[1], swap_sem.at[0], swap_sem.at[1],
                device_id=(z * 2 + 1 - core, pool), device_id_type=MESH,
            )
            swap_copy.start()
        for i in batch:
            wait_bytes(r2.at[i], query_sem.at[i])
            for n in (i, 4 + i):
                kept[n].wait()
                given[n].wait_recv()
        pairs = [(i, s) for i in batch for s in range(4)]
        arrived = {i: r2[i].astype(F32).reshape(2, 4, 8, 128) for i in batch}
        queries = [arrived[i][:, s].reshape(16, 128).astype(BF16) for i, s in pairs]
        scores = []
        blank = jnp.zeros((16, 128), BF16)
        for n in range(0, len(pairs), 2):
            i, s = pairs[n]
            both = jnp.concatenate(
                [
                    jnp.concatenate([queries[n], blank], axis=1),
                    jnp.concatenate([blank, queries[n + 1]], axis=1),
                ],
                axis=0,
            )
            found = jnp.concatenate(
                [
                    lax.dot_general(
                        both, jnp.concatenate([kc[i, c, s], kc[i, c, s + 1]], axis=1), ACROSS,
                        preferred_element_type=F32,
                    )
                    for c in range(2)
                ],
                axis=1,
            ) * scale
            scores += [found[:16], found[16:]]
        tops = [
            jnp.max(jnp.where(valid[s], x, NEGATIVE), axis=1, keepdims=True)
            for x, (_, s) in zip(scores, pairs)
        ]
        weights = [
            jnp.where(valid[s], jnp.exp(x - top), 0.0) for x, top, (_, s) in zip(scores, tops, pairs)
        ]
        bottoms = [jnp.sum(x, axis=1, keepdims=True) for x in weights]
        weights = [x.astype(BF16) for x in weights]
        sums = [
            jnp.dot(x, vc[i, :, s].reshape(768, 128), preferred_element_type=F32)
            for x, (i, s) in zip(weights, pairs)
        ]
        for n, i in enumerate(batch):
            mine = slice(4 * n, 4 * n + 4)
            for c in range(2):
                half = slice(8 * c, 8 * c + 8)
                top = jnp.concatenate([x[half] for x in tops[mine]], axis=0)
                bottom = jnp.concatenate([x[half] for x in bottoms[mine]], axis=0)
                row = jnp.where(row32 == lane32, top, 0.0) + jnp.where(row32 + 32 == lane32, bottom, 0.0)
                st4[i, c] = jnp.sum(row, axis=0, keepdims=True)
                s4[i, c] = jnp.concatenate([x[half] for x in sums[mine]], axis=0).astype(BF16)
        for i in batch:
            chip = lax.rem(z + core + 2 * i, 8)
            slot = lax.rem(8 - core - 2 * i + 8, 8)
            for c in range(2):
                remote = [
                    pltpu.make_async_remote_copy(
                        src.at[i, c], dst.at[slot], send_sem.at[phase], recv_sem.at[phase],
                        device_id=(chip * 2 + c, pool), device_id_type=MESH,
                    )
                    for src, dst, phase in ((st4, rt4, 3), (s4, r4, 4))
                ]
                if i or c:
                    for copy in remote:
                        copy.start()
                else:

                    @pl.when(core == 1)
                    def _(remote=remote):
                        for copy in remote:
                            copy.start()

                    @pl.when(core == 0)
                    def _():
                        pltpu.make_async_copy(st4.at[0, 0], rt4.at[0], recv_sem.at[3]).start()
                        pltpu.make_async_copy(s4.at[0, 0], r4.at[0], recv_sem.at[4]).start()

    swap_copy.wait()
    there = swap[1]
    lane4 = lax.broadcasted_iota(jnp.int32, (4, 128), 1)
    here_turned, there_turned = pltpu.roll(here, 64, 1), pltpu.roll(there, 64, 1)
    first = core == 0
    key_raw = jnp.where(lane4 < 64, jnp.where(first, here, there), jnp.where(first, there_turned, here_turned))
    value_raw = jnp.where(lane4 < 64, jnp.where(first, here_turned, there_turned), jnp.where(first, there, here))
    key_new = rotate(key_raw, slice(0, 4)).astype(BF16).astype(F32)
    value_new = value_raw.astype(BF16).astype(F32)

    def spread(x):
        return jnp.concatenate([jnp.broadcast_to(x[s : s + 1], (8, 128)) for s in range(4)], axis=0)

    own = jnp.sum(query.astype(F32) * spread(key_new), axis=1, keepdims=True) * scale
    own = jnp.sum(jnp.where(row32 == lane32, own, 0.0), axis=0, keepdims=True)

    wait_bytes(rt4, recv_sem.at[3])
    parts = jnp.concatenate([rt4[i] for i in range(8)], axis=0)
    largest = jnp.maximum(jnp.max(parts, axis=0, keepdims=True), own)
    factor = jnp.exp(parts - largest)
    own_weight = jnp.exp(own - largest)
    denominator = jnp.sum(factor * pltpu.roll(parts, 96, 1), axis=0, keepdims=True) + own_weight
    shares = jnp.concatenate(
        [factor / denominator, own_weight.astype(BF16).astype(F32) / denominator, jnp.zeros((7, 128), F32)], axis=0
    ).T
    attention = shares[:32, 8:9] * spread(value_new)
    wait_bytes(r4, recv_sem.at[4])
    for i in range(8):
        attention = attention + shares[:32, i : i + 1] * r4[i].astype(F32)
    attention = attention.astype(BF16)

    s5[...] = attention
    for i, offset in enumerate(POOL_OFFSETS):
        pltpu.make_async_remote_copy(
            s5, r5.at[i], send_sem.at[5], recv_sem.at[5 if i < FAR_ROWS else 8],
            device_id=(head, pool_peer(offset)), device_id_type=MESH,
        ).start()
    later[3].wait()
    last.wait()

    def place_rows(source, block):
        x5[pl.ds(pl.multiple_of(source * 32, 32), 32), :] = block.astype(F32)

    place_rows(pool, s5[...])
    wait_bytes(r5.at[pl.ds(FAR_ROWS, 15 - FAR_ROWS)], recv_sem.at[8])
    for i in range(FAR_ROWS, 15):
        place_rows(pool_peer([4 - o for o in POOL_OFFSETS[i]]), r5[i])
    wait_bytes(r5.at[pl.ds(0, FAR_ROWS)], recv_sem.at[5])
    for i in range(FAR_ROWS):
        place_rows(pool_peer([4 - o for o in POOL_OFFSETS[i]]), r5[i])
    rows = jnp.concatenate([x5[pl.ds(j, 64, stride=8), :].astype(BF16) for j in range(8)], axis=1)

    part = jnp.dot(rows, wo[...], preferred_element_type=F32)
    for j in range(8):
        x6[:, j, :] = part[:, 128 * j : 128 * j + 128]
    for i, offset in enumerate(OUTPUT_OFFSETS):
        to = head_peer(offset)
        row = [x6[slot_smem[0, to * 4 + k]] for k in range(4)]
        s6[i, :16] = jnp.concatenate(row[:2], axis=0).astype(BF16)
        s6[i, 16:] = jnp.concatenate(row[2:], axis=0).astype(BF16)
        if i < 15:
            head_send(s6.at[i], r6.at[i], 6, recv_sem.at[6 if i < FAR_OUTPUTS else 7], offset)

    wait_bytes(r1, send_sem.at[0])
    wait_bytes(rkv, send_sem.at[1])
    for copy in given:
        copy.wait_send()
    for buf, phase in ((r4, 2), (rt4, 3), (r4, 4)):
        wait_bytes(buf.at[pl.ds(0, 7)], send_sem.at[phase])

        @pl.when(core == 1)
        def _(buf=buf, phase=phase):
            wait_bytes(buf.at[0], send_sem.at[phase])

    wait_bytes(r5, send_sem.at[5])

    mixed = s6[15].astype(F32)
    wait_bytes(r6.at[pl.ds(FAR_OUTPUTS, 15 - FAR_OUTPUTS)], recv_sem.at[7])
    for i in range(FAR_OUTPUTS, 15):
        mixed = mixed + r6[i].astype(F32)
    wait_bytes(r6.at[pl.ds(0, FAR_OUTPUTS)], recv_sem.at[6])
    for i in range(FAR_OUTPUTS):
        mixed = mixed + r6[i].astype(F32)
    out_ref[...] = mixed
    wait_bytes(r6, send_sem.at[6])


def local(hidden_in, w_query, w_key, w_value, w_out, k_cache, v_cache, cache_len, slot_of):
    hbm = pl.BlockSpec(memory_space=pl.ANY)
    vmem = pl.BlockSpec(memory_space=pltpu.VMEM)
    return pl.pallas_call(
        kernel,
        out_shape=pltpu.VMEM((32, 128), F32),
        in_specs=[hbm] * 9,
        out_specs=vmem,
        scratch_shapes=[
            pltpu.VMEM((1, 64), jnp.int32),
            pltpu.VMEM((1, 64), jnp.int32),
            pltpu.SMEM((1, 64), jnp.int32),
            pltpu.VMEM((64, 1024), BF16),
            pltpu.VMEM((1024, 1024), BF16),
            pltpu.VMEM((128, 1024), BF16),
            pltpu.VMEM((1024, 1024), BF16),
            pltpu.VMEM((4, 2, 4, 384, 128), BF16),
            pltpu.VMEM((4, 2, 4, 384, 128), BF16),
            pltpu.VMEM((512, 128), F32),
            pltpu.VMEM((15, 32, 128), F32),
            pltpu.VMEM((16, 4, 128), F32),
            pltpu.VMEM((15, 4, 128), F32),
            pltpu.VMEM((2, 4, 128), F32),
            pltpu.VMEM((32, 128), BF16),
            pltpu.VMEM((4, 2, 32, 128), BF16),
            pltpu.VMEM((4, 2, 32, 128), BF16),
            pltpu.VMEM((8, 32, 128), BF16),
            pltpu.VMEM((4, 2, 1, 128), F32),
            pltpu.VMEM((8, 1, 128), F32),
            pltpu.VMEM((32, 128), BF16),
            pltpu.VMEM((15, 32, 128), BF16),
            pltpu.VMEM((512, 128), F32),
            pltpu.VMEM((64, 8, 128), F32),
            pltpu.VMEM((16, 32, 128), BF16),
            pltpu.VMEM((15, 32, 128), BF16),
            pltpu.SemaphoreType.DMA((11,)),
            pltpu.SemaphoreType.DMA((7,)),
            pltpu.SemaphoreType.DMA((9,)),
            pltpu.SemaphoreType.DMA((4,)),
            pltpu.SemaphoreType.DMA((2,)),
            pltpu.SemaphoreType.DMA((3, 8)),
        ],
        compiler_params=pltpu.CompilerParams(
            collective_id=0, has_side_effects=True, vmem_limit_bytes=63 * 1024 * 1024
        ),
    )(
        hidden_in, w_query, w_key.T, w_value.T, w_out, k_cache, v_cache,
        cache_len.reshape(1, 64), slot_of.reshape(1, 64),
    ).reshape(4, 1024)


def solution(mesh):
    in_specs = (
        P(None, "pool"),
        P("pool", "head"),
        P("pool", "head"),
        P("pool", "head"),
        P("head", "pool"),
        P("pool", "head", None),
        P("pool", "head", None),
        P(),
        P(),
    )
    out_specs = P("head", "pool")
    return jax.shard_map(local, mesh=mesh, in_specs=in_specs, out_specs=out_specs, check_vma=False)
```
